256 devices in a mesh: replica: 32 (over y, z_lo, core), shard: 8 (over x, z_hi).
Axes of the slice: x: 4, y: 4, z: 8 (z_hi: 2, z_lo: 4; z = z_hi * 4 + z_lo), core: 2. Of those that a mesh axis runs over, the one named last changes fastest.
Arguments:
- activations: bfloat16 [262144, 4096], P(('replica', 'shard')), may hold values from -24 to 24
- out_grad: bfloat16 [262144, 512], P(('replica', 'shard')), may hold values from -6 to 6
- master: float32 [4096, 512], P('shard'), may hold values from -6 to 6
- moment_one: float32 [4096, 512], P('shard'), may hold values from -6 to 6
- moment_two: float32 [4096, 512], P('shard'), may hold values from 0.25 to 4
- alive: int32 [32], replicated, may hold values from 0 to 1, as said below
- step_count: int32 [1], replicated, may hold values from 1 to 20
Outputs:
- clipped: float32 [4096, 512], P('shard')
- master_new: float32 [4096, 512], P('shard')
- moment_one_new: float32 [4096, 512], P('shard')
- moment_two_new: float32 [4096, 512], P('shard')
- params: bfloat16 [4096, 512], replicated
The draws below stay inside these ranges and needn't reach their ends.
Inputs may be any that keep to these rules, and one draw needn't show every extreme that they name: `alive`: exactly one replica group is dead (one entry is 0, all others 1).
All inputs are finite; a program needn't handle non-finite values.
Results may differ from the reference program's by a relative error of at most 0.001.
Values may be sent and summed in bfloat16 or wider, within the bound.
A program may use at most 128 MiB of HBM per device.

```python
import math
import jax
import jax.numpy as jnp
from jax import lax

DW = 4096
KVW = 512
TOK_DEV = 1024
TOKENS = 262144
N_REPLICA = 32
N_SHARD = 8


def draw_alive(key, part):
    key = jax.random.fold_in(key, 1)
    dead = jax.random.randint(key, (), 0, N_REPLICA)
    return (jnp.arange(N_REPLICA) != dead).astype(jnp.int32)


def with_spikes(entries, key, source, target, blocks, factor):
    def block_of(position):
        return (jnp.arange(entries.shape[position]) // (entries.shape[position] // blocks)).reshape((-1,) + (1,) * (entries.ndim - 1 - position))

    first = jax.random.permutation(key, blocks)[block_of(target)]
    other_side = (block_of(target) + blocks // 2) % blocks
    return jnp.where((block_of(source) == first) | (block_of(source) == other_side), factor * entries, entries)


def block_levels(own_key, dims, pieces, least, largest):
    def one(axis_at, blocks):
        steps = jax.random.uniform(jax.random.fold_in(jax.random.fold_in(own_key, 6), axis_at), (blocks,), jnp.float32, least / len(pieces), largest / len(pieces))
        return jnp.repeat(jnp.exp(steps), dims[axis_at] // blocks).reshape((-1,) + (1,) * (len(dims) - axis_at - 1))

    gain = one(*pieces[0])
    for cut in pieces[1:]:
        gain = gain * one(*cut)
    return gain


def scatter_about(own_key, extent, width, limit, shards=(), dtype=jnp.bfloat16):
    values = jax.random.normal(own_key, extent, jnp.float32) * width
    if len(shards) > 0:
        values = block_levels(own_key, extent, shards, -0.22, 0.18) * values
    return jnp.clip(values, min=-limit, max=limit).astype(dtype)


def heavy_noise(key, shape, width, reach, cuts, heavy, dtype=jnp.bfloat16):
    values = width * jax.random.normal(key, shape, jnp.float32)
    if cuts:
        values = values * block_levels(key, shape, cuts, -0.22, 0.18)
    return jnp.clip(with_spikes(values, jax.random.fold_in(key, 3), *heavy), -reach, reach).astype(dtype)


def setup_inputs(seed: int = 0) -> dict:
    key_of = jax.random.split(jax.random.key(seed), 8)
    return {
        "activations": heavy_noise(key_of[0], (TOKENS, DW), 1.0, 24.0, ((0, 256),), (0, 1, 256, 6.0)),
        "out_grad": scatter_about(key_of[1], (TOKENS, KVW), 1.0, 6.0, ((0, 256),)),
        "master": scatter_about(key_of[2], (DW, KVW), 1.0, 6.0, ((0, 8),), jnp.float32),
        "moment_one": scatter_about(key_of[3], (DW, KVW), 1.0, 6.0, ((0, 8),), jnp.float32),
        "moment_two": jnp.clip(jnp.exp(math.log(4.0) - 2.7725887 * jax.random.uniform(key_of[4], (DW, KVW), jnp.float32) ** block_levels(key_of[4], (DW, KVW), ((0, 8),), -0.2, 0.2)), 0.25, 4.0),
        "alive": draw_alive(jax.random.fold_in(key_of[7], 71), 0),
        "step_count": jax.random.randint(key_of[6], (1,), 1, 21).astype(jnp.int32),
    }


def reference(activations, out_grad, master, moment_one, moment_two, alive, step_count):
    rows = TOK_DEV * N_SHARD
    blocks_x = activations.reshape(N_REPLICA, rows, DW)
    blocks_y = out_grad.reshape(N_REPLICA, rows, KVW)
    weights = alive.astype(jnp.float32)

    def accumulate(total, item):
        block_x, block_y, weight = item
        term = lax.dot_general(block_x, block_y, (((0,), (0,)), ((), ())), preferred_element_type=jnp.float32)
        return (total + weight * term, None)
    start = jnp.zeros((DW, KVW), jnp.float32)
    grad_sum, unused = lax.scan(accumulate, start, (blocks_x, blocks_y, weights))
    square = jnp.sum(grad_sum * grad_sum)
    factor = jnp.minimum(1.0, jnp.sqrt(jnp.float32(DW * KVW)) / jnp.sqrt(square + 1e-06))
    clipped = grad_sum * factor
    moment_one_new = 0.9 * moment_one + 0.1 * clipped
    moment_two_new = 0.95 * moment_two + 0.05 * clipped * clipped
    steps_done = step_count[0].astype(jnp.float32)
    first_hat = moment_one_new / (1.0 - jnp.power(jnp.float32(0.9), steps_done))
    second_hat = moment_two_new / (1.0 - jnp.power(jnp.float32(0.95), steps_done))
    update = first_hat / (jnp.sqrt(second_hat) + 1e-08) + 0.1 * master
    master_new = master - 0.01 * update
    params = master_new.astype(jnp.bfloat16)
    return (clipped, master_new, moment_one_new, moment_two_new, params)
```

```python
import functools

import jax
import jax.numpy as jnp
from jax import lax
from jax.experimental import pallas as pl
from jax.experimental.pallas import tpu as pltpu
from jax.sharding import PartitionSpec as P

DW = 4096
KVW = 512
TOK = 1024
SH = 512
HALF = 256
F32 = jnp.float32
BF16 = jnp.bfloat16
I16 = jnp.int16
MESH = pl.DeviceIdType.MESH
LEVELS = 32000.0


def place():
    r = lax.axis_index("replica")
    s = lax.axis_index("shard")
    return s // 2, r // 8, (s % 2) * 4 + (r // 2) % 4, r % 2


def dev(x, y, z, c):
    return ((y * 4 + z % 4) * 2 + c, x * 2 + z // 4)


def remote(src, dst, ssem, rsem, who):
    return pltpu.make_async_remote_copy(
        src_ref=src, dst_ref=dst, send_sem=ssem, recv_sem=rsem, device_id=who, device_id_type=MESH
    )


def code_of(largest):
    code = jnp.ceil(8.0 * jnp.log2(jnp.maximum(largest, 1e-37) * (1.0 / LEVELS)))
    return jnp.clip(code, -960.0, 960.0)


def step_of(code):
    return jnp.exp2(code * 0.125)


def fold_max(acc, block):
    rows, cols = block.shape
    return jnp.maximum(acc, jnp.max(jnp.abs(block).reshape(rows // 8, 8, cols), axis=0))


def encode(read, q, rows, cols, chunk, largest=None):
    if largest is None:
        largest = lax.fori_loop(
            0, rows // chunk, lambda i, acc: fold_max(acc, read(pl.multiple_of(i * chunk, chunk))),
            jnp.zeros((8, cols), F32))
    code = code_of(jnp.max(largest, axis=0, keepdims=True))
    inverse = step_of(-code)

    @pl.loop(0, rows // chunk)
    def _(i):
        at = pl.multiple_of(i * chunk, chunk)
        q[pl.ds(at, chunk), :] = jnp.round(read(at) * inverse).astype(jnp.int32).astype(I16)

    q[pl.ds(rows, 16), :] = jnp.broadcast_to(code.astype(jnp.int32), (16, cols)).astype(I16)


def steps_in(q, rows):
    return step_of(q[pl.ds(rows, 16), :].astype(jnp.int32).astype(F32)[0:1, :])


def decoded(q, at, chunk, step):
    return q[pl.ds(at, chunk), :].astype(jnp.int32).astype(F32) * step


def kernel(act, grad, master, m1, m2, alive, steps, clipped_o, master_o, m1_o, m2_o, params,
           a, b, w0, w1, w2, own, psend, precv, q1s, q1r, q1sy, q1ry, sum1, sum1y, q2s, q2r, sum2, q3s, q3r,
           block, gq, nz, ny, nx, nc,
           asem, csem_s, csem_r, s1s, s1r, s2s, s2r, s3s, s3r, ns, nr, gs, gr, ps, pr, ks, kr):
    x, y, z, c = place()
    zh, zl = z // 4, z % 4
    peer = dev(x, y, z, 1 - c)

    def at_x(k):
        return dev((x + k) % 4, y, z, c)

    def at_y(k):
        return dev(x, (y + k) % 4, z, c)

    def at_z(k):
        return dev(x, y, (z + k) % 8, c)

    barrier = pltpu.get_barrier_semaphore()
    pl.semaphore_signal(barrier, inc=1, device_id=peer, device_id_type=MESH)
    for k in range(1, 4):
        pl.semaphore_signal(barrier, inc=1, device_id=at_x(k), device_id_type=MESH)
        pl.semaphore_signal(barrier, inc=1, device_id=at_y(k), device_id_type=MESH)
    for k in range(1, 8):
        pl.semaphore_signal(barrier, inc=1, device_id=at_z(k), device_id_type=MESH)

    b_copy = pltpu.make_async_copy(grad, b, asem.at[8])
    b_copy.start()

    def a_copy(i, h):
        s = ((x + i + 1) % 4) * 2 + h
        cols = pl.ds(pl.multiple_of(s * SH, SH), SH)
        return pltpu.make_async_copy(act.at[:, cols], a.at[:, cols], asem.at[i * 2 + h])

    for i in range(4):
        for h in range(2):
            a_copy(i, h).start()
    state = [pltpu.make_async_copy(master, w0, asem.at[9]), pltpu.make_async_copy(m1, w1, asem.at[10]),
             pltpu.make_async_copy(m2, w2, asem.at[11])]
    for copy in state:
        copy.start()
    b_copy.wait()
    weight = alive[lax.axis_index("replica")].astype(F32)
    b[...] = (b[...].astype(F32) * weight).astype(BF16)

    def core_copy(i, h):
        return remote(psend.at[i, h], precv.at[i, h], csem_s.at[i * 2 + h], csem_r.at[i * 2 + h], peer)

    def first_x(i):
        return remote(q1s.at[i], q1r.at[i], s1s.at[i], s1r.at[i], at_x(i + 1))

    def first_y(i, j):
        return remote(q1sy.at[i, j], q1ry.at[i, j], s1s.at[i * 3 + j], s1r.at[i * 3 + j], at_y(j + 1))

    pl.semaphore_wait(barrier, 14)

    def product(i):
        @pl.loop(0, 2)
        def _(h):
            s = ((x + i + 1) % 4) * 2 + h
            a_copy(i, h).wait()

            def term(half):
                cols = pl.ds(pl.multiple_of(s * SH + half * HALF, HALF), HALF)
                return lax.dot_general(a[:, cols], b[...], (((0,), (0,)), ((), ())), preferred_element_type=F32)

            psend[i, h] = term(1 - c)
            core_copy(i, h).start()
            own[i, h] = term(c)

    def combine(i):
        core_copy(i, 0).wait_recv()
        core_copy(i, 1).wait_recv()

        def add(t, acc):
            h, at = t // 4, pl.multiple_of((t % 4) * 64, 64)
            total = own[i, h, pl.ds(at, 64), :] + precv[i, h, pl.ds(at, 64), :]
            own[i, h, pl.ds(at, 64), :] = total
            return fold_max(acc, total)

        largest = lax.fori_loop(0, 8, add, jnp.zeros((8, KVW), F32))

        def read(at):
            return own[i, at // HALF, pl.ds(pl.multiple_of(at % HALF, 32), 32), :]

        @pl.when(jnp.logical_and(c == 0, i < 3))
        def _():
            encode(read, q1s.at[i], 512, KVW, 32, largest)
            first_x(i).start()

        @pl.when(c == 1)
        def _():
            precv[i, 0, 0:8, :] = largest
            for j in range(3):
                cols = pl.ds(pl.multiple_of(((y + j + 1) % 4) * 128, 128), 128)

                def read_y(at):
                    return own[i, at // HALF, pl.ds(pl.multiple_of(at % HALF, 128), 128), cols]

                encode(read_y, q1sy.at[i, j], 512, 128, 128, precv[i, 0, 0:8, cols])
                first_y(i, j).start()

    @pl.loop(0, 5)
    def _(i):
        @pl.when(i < 4)
        def _():
            product(i)

        @pl.when(i > 0)
        def _():
            combine(i - 1)

    @pl.when(c == 0)
    def _():
        for i in range(3):
            first_x(i).wait_recv()
        step = [steps_in(q1r.at[i], 512) for i in range(3)]

        @pl.loop(0, 16)
        def _(t):
            at = pl.multiple_of(t * 32, 32)
            total = own[3, t // 8, pl.ds(pl.multiple_of((t % 8) * 32, 32), 32), :]
            for i in range(3):
                total += decoded(q1r.at[i], at, 32, step[i])
            for k in range(4):
                sum1[k, pl.ds(at, 32), :] = total[:, k * 128:(k + 1) * 128]

    @pl.when(c == 1)
    def _():
        mine = pl.ds(pl.multiple_of(y * 128, 128), 128)

        @pl.loop(0, 4)
        def _(i):
            for j in range(3):
                first_y(i, j).wait_recv()
            step = [steps_in(q1ry.at[i, j], 512) for j in range(3)]

            @pl.loop(0, 4)
            def _(t):
                at = pl.multiple_of(t * 128, 128)
                total = own[i, t // 2, pl.ds(pl.multiple_of((t % 2) * 128, 128), 128), mine]
                for j in range(3):
                    total += decoded(q1ry.at[i, j], at, 128, step[j])
                sum1[i, pl.ds(at, 128), :] = total

    def second(j):
        k = j + 1
        xx = jnp.where(c == 0, x, (x + k) % 4)
        yy = jnp.where(c == 0, (y + k) % 4, y)
        return remote(q2s.at[j], q2r.at[j], s2s.at[j], s2r.at[j], dev(xx, yy, z, c))

    @pl.loop(0, 3)
    def _(j):
        slot = jnp.where(c == 0, (y + j + 1) % 4, j)
        encode(lambda at: sum1[slot, pl.ds(at, 128), :], q2s.at[j], 512, 128, 128)
        second(j).start()

    for j in range(3):
        second(j).wait_recv()
    step2 = [steps_in(q2r.at[j], 512) for j in range(3)]
    slot2 = jnp.where(c == 0, y, 3)

    @pl.loop(0, 4)
    def _(t):
        at = pl.multiple_of(t * 128, 128)
        total = sum1[slot2, pl.ds(at, 128), :]
        for j in range(3):
            total += decoded(q2r.at[j], at, 128, step2[j])
        sum2[pl.ds(at, 128), :] = total

    def third(k):
        return remote(q3s.at[k - 1], q3r.at[k - 1], s3s.at[k - 1], s3r.at[k - 1], at_z(k))

    for k in range(1, 8):
        rows = pl.ds(pl.multiple_of(((z + k) % 8) * 64, 64), 64)
        encode(lambda at: sum2[rows, :], q3s.at[k - 1], 64, 128, 64)
        third(k).start()
    total = sum2[pl.ds(pl.multiple_of(z * 64, 64), 64), :]
    for k in range(1, 8):
        third(k).wait_recv()
        total += decoded(q3r.at[k - 1], 0, 64, steps_in(q3r.at[k - 1], 64))
    block[...] = total

    mine = gq.at[c, y, zl]
    encode(lambda at: block[...], mine, 64, 128, 64)

    def group_z(k):
        return remote(mine, mine, gs.at[k - 1], gr.at[k - 1], dev(x, y, zh * 4 + (zl + k) % 4, c))

    def group_y(k):
        return remote(gq.at[c, y], gq.at[c, y], gs.at[k + 2], gr.at[k + 2], at_y(k))

    group_c = remote(gq.at[c], gq.at[c], gs.at[6], gr.at[6], peer)

    def tell(buf, me, sem, who):
        return remote(buf.at[me], buf.at[me], ns.at[sem], nr.at[sem], who)

    final = decoded(mine, 0, 64, steps_in(mine, 64))
    nz[z] = jnp.sum((final * final).reshape(8, 8, 128), axis=0)
    for k in range(1, 8):
        tell(nz, z, k - 1, at_z(k)).start()
    for k in range(1, 4):
        group_z(k).start()
    for k in range(1, 8):
        tell(nz, z, k - 1, at_z(k)).wait_recv()
    ny[y] = jnp.sum(nz[...], axis=0)
    for k in range(1, 4):
        tell(ny, y, 6 + k, at_y(k)).start()
    for k in range(1, 4):
        group_z(k).wait_recv()
    for k in range(1, 4):
        group_y(k).start()
    for k in range(1, 4):
        tell(ny, y, 6 + k, at_y(k)).wait_recv()
    nx[x] = jnp.sum(ny[...], axis=0)
    for k in range(1, 4):
        tell(nx, x, 9 + k, at_x(k)).start()
    for k in range(1, 4):
        group_y(k).wait_recv()
    group_c.start()
    for k in range(1, 4):
        tell(nx, x, 9 + k, at_x(k)).wait_recv()
    nc[c] = jnp.sum(nx[...], axis=0)
    tell(nc, c, 13, peer).start()
    for copy in state:
        copy.wait()
    group_c.wait_recv()
    tell(nc, c, 13, peer).wait_recv()
    square = jnp.sum(nc[0] + nc[1], keepdims=True)
    factor = jnp.minimum(1.0, jnp.sqrt(F32(DW * KVW)) / jnp.sqrt(square + 1e-06))

    done = jnp.full((1, 128), steps[0].astype(F32))
    correct1 = 1.0 / (1.0 - jnp.exp(done * jnp.log(F32(0.9))))
    correct2 = 1.0 / (1.0 - jnp.exp(done * jnp.log(F32(0.95))))
    s = x * 2 + zh

    @pl.loop(0, 32)
    def _(t):
        cc, yy, zz = t // 16, (t // 4) % 4, t % 4
        q = gq.at[cc, yy, zz]
        clipped = decoded(q, 0, 64, steps_in(q, 64)) * factor
        rows = pl.ds(pl.multiple_of(cc * HALF + zz * 64, 64), 64)
        cols = pl.ds(pl.multiple_of(yy * 128, 128), 128)
        clipped_o[rows, cols] = clipped
        m1_new = 0.9 * w1[rows, cols] + 0.1 * clipped
        m2_new = 0.95 * w2[rows, cols] + 0.05 * clipped * clipped
        m1_o[rows, cols] = m1_new
        m2_o[rows, cols] = m2_new
        old = w0[rows, cols]
        update = (m1_new * correct1) / (jnp.sqrt(m2_new * correct2) + 1e-08) + 0.1 * old
        new = old - 0.01 * update
        master_o[rows, cols] = new
        there = pl.ds(pl.multiple_of(s * SH + cc * HALF + zz * 64, 64), 64)
        params[there, cols] = new.astype(BF16)

    def half(shard):
        return pl.ds(pl.multiple_of(shard * SH + c * HALF, HALF), HALF)

    def col(yy):
        return pl.ds(pl.multiple_of(yy * 128, 128), 128)

    def whole_to(shard, sem, who):
        ref = params.at[half(shard), :]
        return remote(ref, ref, ps.at[sem], pr.at[sem], who)

    def piece_to(shard, sem, who):
        ref = params.at[half(shard), col(y)]
        return remote(ref, ref, ps.at[sem], pr.at[sem], who)

    def to_peer(shard, sem):
        ref = params.at[half(shard), :]
        return remote(ref, ref, ks.at[sem], kr.at[sem], peer)

    other = x * 2 + (1 - zh)

    def shard_at(k, hh):
        return ((x + k) % 4) * 2 + hh

    cross = piece_to(s, 0, at_z(4))
    cross.start()

    @pl.when(c == 0)
    def _():
        for k in range(1, 4):
            whole_to(s, k, at_x(k)).start()
        cross.wait_recv()
        for k in range(1, 4):
            piece_to(other, 3 + k, at_y(k)).start()
        for k in range(1, 4):
            whole_to(s, k, at_x(k)).wait_recv()
            to_peer(shard_at(4 - k, zh), k - 1).start()
        for k in range(1, 4):
            piece_to(other, 3 + k, at_y(k)).wait_recv()
        for k in range(1, 4):
            whole_to(other, 6 + k, at_x(k)).start()
        to_peer(other, 3).start()
        for k in range(1, 4):
            whole_to(other, 6 + k, at_x(k)).wait_recv()
            to_peer(shard_at(4 - k, 1 - zh), 3 + k).start()
        for k in range(1, 4):
            whole_to(s, k, at_x(k)).wait_send()
            piece_to(other, 3 + k, at_y(k)).wait_send()
            whole_to(other, 6 + k, at_x(k)).wait_send()

    @pl.when(c == 1)
    def _():
        def spread(shard, n):
            for k in range(1, 4):
                piece_to(shard, 7 + n * 3 + k - 1, at_y(k)).start()

        def gathered(shard, n):
            for k in range(1, 4):
                piece_to(shard, 7 + n * 3 + k - 1, at_y(k)).wait_recv()
            to_peer(shard, n).start()

        for k in range(1, 4):
            piece_to(s, k, at_x(k)).start()
        for k in range(1, 4):
            piece_to(s, k, at_x(k)).wait_recv()
            spread(shard_at(4 - k, zh), k - 1)
        cross.wait_recv()
        for k in range(1, 4):
            piece_to(other, 3 + k, at_x(k)).start()
        spread(other, 3)
        for k in range(1, 4):
            piece_to(other, 3 + k, at_x(k)).wait_recv()
            spread(shard_at(4 - k, 1 - zh), 3 + k)
        for k in range(1, 4):
            gathered(shard_at(4 - k, zh), k - 1)
        gathered(other, 3)
        for k in range(1, 4):
            gathered(shard_at(4 - k, 1 - zh), 3 + k)
        for k in range(1, 4):
            piece_to(s, k, at_x(k)).wait_send()
            piece_to(other, 3 + k, at_x(k)).wait_send()
        for n in range(7):
            for k in range(1, 4):
                piece_to(s, 7 + n * 3 + k - 1, at_y(k)).wait_send()

    cross.wait_send()
    for n in range(7):
        to_peer(s, n).wait_recv()
        to_peer(s, n).wait_send()

    for i in range(4):
        for h in range(2):
            core_copy(i, h).wait_send()

    @pl.when(c == 0)
    def _():
        for i in range(3):
            first_x(i).wait_send()

    @pl.when(c == 1)
    def _():
        for i in range(4):
            for j in range(3):
                first_y(i, j).wait_send()

    for j in range(3):
        second(j).wait_send()
    for k in range(1, 8):
        third(k).wait_send()
        tell(nz, z, k - 1, at_z(k)).wait_send()
    for k in range(1, 4):
        tell(ny, y, 6 + k, at_y(k)).wait_send()
        tell(nx, x, 9 + k, at_x(k)).wait_send()
        group_z(k).wait_send()
        group_y(k).wait_send()
    tell(nc, c, 13, peer).wait_send()
    group_c.wait_send()


def shards(activations, out_grad, master, moment_one, moment_two, alive, step_count):
    hbm = pl.BlockSpec(memory_space=pl.ANY)
    smem = pl.BlockSpec(memory_space=pltpu.SMEM)
    dma = pltpu.SemaphoreType.DMA
    vm = pltpu.VMEM
    return pl.pallas_call(
        kernel,
        out_shape=[OUT((SH, KVW), F32)] * 4 + [OUT((DW, KVW), BF16)],
        in_specs=[hbm] * 5 + [smem] * 2,
        out_specs=[pl.BlockSpec(memory_space=pltpu.VMEM)] * 5,
        scratch_shapes=[
            vm((TOK, DW), BF16), vm((TOK, KVW), BF16),
            vm((SH, KVW), F32), vm((SH, KVW), F32), vm((SH, KVW), F32),
            vm((4, 2, HALF, KVW), F32), vm((4, 2, HALF, KVW), F32), vm((4, 2, HALF, KVW), F32),
            vm((3, 528, KVW), I16), vm((3, 528, KVW), I16),
            vm((4, 3, 528, 128), I16), vm((4, 3, 528, 128), I16),
            vm((4, 512, 128), F32), vm((8, 128), F32),
            vm((3, 528, 128), I16), vm((3, 528, 128), I16), vm((512, 128), F32),
            vm((7, 80, 128), I16), vm((7, 80, 128), I16),
            vm((64, 128), F32), vm((2, 4, 4, 80, 128), I16),
            vm((8, 8, 128), F32), vm((4, 8, 128), F32), vm((4, 8, 128), F32), vm((2, 8, 128), F32),
            dma((12,)), dma((8,)), dma((8,)), dma((12,)), dma((12,)), dma((3,)), dma((3,)), dma((7,)), dma((7,)),
            dma((14,)), dma((14,)), dma((7,)), dma((7,)), dma((28,)), dma((28,)), dma((7,)), dma((7,)),
        ],
        compiler_params=pltpu.CompilerParams(
            collective_id=0, has_side_effects=True, vmem_limit_bytes=48 * 2**20),
        name="reduce_update_gather",
    )(activations, out_grad, master, moment_one, moment_two, alive, step_count)


OUT = pltpu.VMEM


def solution(mesh):
    return jax.shard_map(
        shards,
        mesh=mesh,
        in_specs=(
            P(("replica", "shard"), None),
            P(("replica", "shard"), None),
            P("shard", None),
            P("shard", None),
            P("shard", None),
            P(),
            P(),
        ),
        out_specs=(P("shard", None), P("shard", None), P("shard", None), P("shard", None), P()),
        check_vma=False,
    )
```

```python
import functools

import jax
import jax.numpy as jnp
from jax import lax
from jax.experimental import pallas as pl
from jax.experimental.pallas import tpu as pltpu
from jax.sharding import PartitionSpec as P

DW = 4096
KVW = 512
TOK = 1024
SH = 512
HALF = 256
QR = HALF + 16
LEVELS = 32000.0
F32 = jnp.float32
BF16 = jnp.bfloat16
I16 = jnp.int16
MESH = pl.DeviceIdType.MESH


def place():
    r = lax.axis_index("replica")
    s = lax.axis_index("shard")
    return s // 2, r // 8, (s % 2) * 4 + (r // 2) % 4, r % 2


def dev(x, y, z, c):
    return ((y * 4 + z % 4) * 2 + c, x * 2 + z // 4)


def remote(src, dst, ssem, rsem, who):
    return pltpu.make_async_remote_copy(
        src_ref=src, dst_ref=dst, send_sem=ssem, recv_sem=rsem, device_id=who, device_id_type=MESH
    )


def span(start, size):
    return pl.ds(pl.multiple_of(start, size), size)


def step_of(code):
    return jnp.exp2(code * 0.125)


def fold_max(acc, block):
    rows, cols = block.shape
    return jnp.maximum(acc, jnp.max(jnp.abs(block).reshape(rows // 8, 8, cols), axis=0))


def encode(read, q, rows, cols, chunk, largest):
    top = jnp.max(largest, axis=0, keepdims=True)
    code = jnp.clip(jnp.ceil(8.0 * jnp.log2(jnp.maximum(top, 1e-37) * (1.0 / LEVELS))), -960.0, 960.0)
    inverse = step_of(-code)

    @pl.loop(0, rows // chunk)
    def _(i):
        at = pl.multiple_of(i * chunk, chunk)
        q[pl.ds(at, chunk), :] = jnp.round(read(at) * inverse).astype(jnp.int32).astype(I16)

    q[pl.ds(rows, 16), :] = jnp.broadcast_to(code.astype(jnp.int32), (16, cols)).astype(I16)


def step_in(q, rows):
    return step_of(q[pl.ds(rows, 16), :].astype(jnp.int32).astype(F32)[0:1, :])


def decoded(q, at, chunk, step):
    return q[pl.ds(at, chunk), :].astype(jnp.int32).astype(F32) * step


def kernel(act, grad, master, m1, m2, alive, steps, clipped_o, master_o, m1_o, m2_o, params,
           a, b, w0, w1, w2, ow, g, got, q1s, q1rx, q1ry, q2x, q2y, q2r, full, part, q3s, q3r, block, gq, oq,
           nz, nxy, nc, asem, cs, cr, s1s, s1r, s2s, s2r, s3s, s3r, os, orr, ns, nr, gs, gr, ps, pr, ks, kr):
    x, y, z, c = place()
    zh, zl = z // 4, z % 4
    peer = dev(x, y, z, 1 - c)
    shard = x * 2 + zh
    other = x * 2 + 1 - zh
    left = []

    def at_x(k):
        return dev((x + k) % 4, y, z, c)

    def at_y(k):
        return dev(x, (y + k) % 4, z, c)

    def at_z(k):
        return dev(x, y, (z + k) % 8, c)

    def at_zl(k, h):
        return dev(x, y, (zh if h else 1 - zh) * 4 + (zl + k) % 4, c)

    xy = [(i, j) for i in range(4) for j in range(4) if (i, j) != (0, 0)]

    def at_xy(k):
        return dev((x + xy[k][0]) % 4, (y + xy[k][1]) % 4, z, c)

    barrier = pltpu.get_barrier_semaphore()
    pl.semaphore_signal(barrier, inc=1, device_id=peer, device_id_type=MESH)
    for k in range(15):
        pl.semaphore_signal(barrier, inc=1, device_id=at_xy(k), device_id_type=MESH)
    for k in range(1, 8):
        pl.semaphore_signal(barrier, inc=1, device_id=at_z(k), device_id_type=MESH)

    def a_copy(t):
        cols = span((((x + t % 4 + 1) % 4) * 2 + jnp.where(t < 4, 1 - zh, zh)) * SH, SH)
        return pltpu.make_async_copy(act.at[:, cols], a.at[:, cols], asem.at[t])

    b_copy = pltpu.make_async_copy(grad, b, asem.at[8])
    b_copy.start()
    for t in range(8):
        a_copy(t).start()
    state = [pltpu.make_async_copy(src, dst, asem.at[9 + n]) for n, (src, dst) in
             enumerate(((master, w0), (m1, w1), (m2, w2)))]
    for copy in state:
        copy.start()
    b_copy.wait()
    weight = alive[lax.axis_index("replica")].astype(F32)
    b[...] = (b[...].astype(F32) * weight).astype(BF16)

    def core_copy(t):
        return remote(g.at[t, span((1 - c) * HALF, HALF), :], got.at[t], cs.at[t], cr.at[t], peer)

    def product(t):
        a_copy(t).wait()
        cols = span((((x + t % 4 + 1) % 4) * 2 + jnp.where(t < 4, 1 - zh, zh)) * SH, SH)
        g[t] = lax.dot_general(a[:, cols], b[...], (((0,), (0,)), ((), ())), preferred_element_type=F32)

    def first_x(t):
        return remote(q1s.at[t], q1rx.at[t], s1s.at[t * 3], s1r.at[t * 3], at_x(t % 4 + 1))

    def first_y(t, j):
        return remote(q1s.at[t, :, span(((y + j + 1) % 4) * 128, 128)], q1ry.at[t * 3 + j], s1s.at[t * 3 + j],
                      s1r.at[t * 3 + j], at_y(j + 1))

    def combine(t):
        core_copy(t).wait_recv()

        def add(n, acc):
            rows = span(c * HALF + n * 64, 64)
            total = g[t, rows, :] + got[t, span(n * 64, 64), :]
            g[t, rows, :] = total
            return fold_max(acc, total)

        largest = lax.fori_loop(0, 4, add, jnp.zeros((8, KVW), F32))

        @pl.when(jnp.logical_or(c == 1, t % 4 < 3))
        def _():
            encode(lambda at: g[t, span(c * HALF + at, 32), :], q1s.at[t], HALF, KVW, 32, largest)

        @pl.when(jnp.logical_and(c == 0, t % 4 < 3))
        def _():
            first_x(t).start()

        @pl.when(c == 1)
        def _():
            for j in range(3):
                first_y(t, j).start()

    product(0)
    pl.semaphore_wait(barrier, 23)
    core_copy(0).start()
    piece = (span(c * HALF, HALF), span(y * 128, 128))
    lend = [remote(src.at[piece[0], piece[1]], ow.at[n], os.at[n], orr.at[n], at_z(4)) for n, src in
            enumerate((master, m1, m2))]
    for copy in lend:
        copy.start()
        left.append(copy.wait_send)

    @pl.loop(1, 10)
    def _(t):
        @pl.when(t < 8)
        def _():
            product(t)
            core_copy(t).start()

        @pl.when(t > 1)
        def _():
            combine(t - 2)

    @left.append
    def _():
        @pl.loop(0, 8)
        def _(t):
            core_copy(t).wait_send()

        @pl.when(c == 0)
        def _():
            for t in (0, 1, 2, 4, 5, 6):
                first_x(t).wait_send()

        @pl.when(c == 1)
        def _():
            @pl.loop(0, 8)
            def _(t):
                for j in range(3):
                    first_y(t, j).wait_send()

    def second_y(h, j):
        return remote(q2x.at[h, :, span(((y + j + 1) % 4) * 128, 128)], q2r.at[h, j], s2s.at[h * 3 + j],
                      s2r.at[h * 3 + j], at_y(j + 1))

    def second_x(h, i):
        return remote(q2y.at[h, i], q2r.at[h, i], s2s.at[h * 3 + i], s2r.at[h * 3 + i], at_x(i + 1))

    def first_sums(h):
        @pl.when(c == 0)
        def _():
            for i in range(3):
                first_x(h * 4 + i).wait_recv()
            step = [step_in(q1rx.at[h * 4 + i], HALF) for i in range(3)]

            def add(n, acc):
                at = pl.multiple_of(n * 32, 32)
                total = g[h * 4 + 3, pl.ds(at, 32), :]
                for i in range(3):
                    total += decoded(q1rx.at[h * 4 + i], at, 32, step[i])
                full[pl.ds(at, 32), :] = total
                return fold_max(acc, total)

            largest = lax.fori_loop(0, HALF // 32, add, jnp.zeros((8, KVW), F32))
            encode(lambda at: full[pl.ds(at, 32), :], q2x.at[h], HALF, KVW, 32, largest)
            for j in range(3):
                second_y(h, j).start()
            part[h] = full[:, span(y * 128, 128)]

        @pl.when(c == 1)
        def _():
            @pl.loop(0, 4)
            def _(i):
                t = h * 4 + i
                for j in range(3):
                    first_y(t, j).wait_recv()
                step = [step_in(q1ry.at[t * 3 + j], HALF) for j in range(3)]

                def add(n, acc):
                    at = pl.multiple_of(n * 128, 128)
                    total = g[t, pl.ds(pl.multiple_of(HALF + at, 128), 128), span(y * 128, 128)]
                    for j in range(3):
                        total += decoded(q1ry.at[t * 3 + j], at, 128, step[j])
                    part[h, pl.ds(at, 128), :] = total
                    return fold_max(acc, total)

                largest = lax.fori_loop(0, 2, add, jnp.zeros((8, 128), F32))

                @pl.when(i < 3)
                def _():
                    encode(lambda at: part[h, pl.ds(at, 128), :], q2y.at[h, i], HALF, 128, 128, largest)
                    second_x(h, i).start()

    def third(h, k):
        n = h * 4 + k
        return remote(q3s.at[n], q3r.at[n], s3s.at[n], s3r.at[n], at_zl(k, h))

    def second_sums(h):
        for j in range(3):
            second_y(h, j).wait_recv()
        step = [step_in(q2r.at[h, j], HALF) for j in range(3)]
        for n in range(2):
            at = n * 128
            total = part[h, at:at + 128, :]
            for j in range(3):
                total += decoded(q2r.at[h, j], at, 128, step[j])
            part[h, at:at + 128, :] = total
        for k in range(h, 4):
            rows = span(((zl + k) % 4) * 64, 64)
            data = part[h, rows, :]
            encode(lambda at: data, q3s.at[h * 4 + k], 64, 128, 64, fold_max(jnp.zeros((8, 128), F32), data))
            third(h, k).start()
            left.append(third(h, k).wait_send)

    @left.append
    def _():
        for h in range(2):
            for j in range(3):
                second_y(h, j).wait_send()

    first_sums(0)
    second_sums(0)
    first_sums(1)
    second_sums(1)
    total = part[1, span(zl * 64, 64), :]
    for h, k in [(0, 0), (0, 1), (0, 2), (0, 3), (1, 1), (1, 2), (1, 3)]:
        third(h, k).wait_recv()
        total += decoded(q3r.at[h * 4 + k], 0, 64, step_in(q3r.at[h * 4 + k], 64))

    mine = gq.at[c, y, zl]
    encode(lambda at: total, mine, 64, 128, 64, fold_max(jnp.zeros((8, 128), F32), total))
    final = decoded(mine, 0, 64, step_in(mine, 64))

    def tell_z(k):
        return remote(nz.at[z], nz.at[z], ns.at[k - 1], nr.at[k - 1], at_z(k))

    def tell_xy(k):
        slot = nxy.at[x * 4 + y]
        return remote(slot, slot, ns.at[7 + k], nr.at[7 + k], at_xy(k))

    tell_c = remote(nc.at[c], nc.at[c], ns.at[22], nr.at[22], peer)

    def group_z(k):
        return remote(mine, mine, gs.at[k], gr.at[k], at_zl(k, 1))

    def cross_z(k):
        return remote(mine, oq.at[zl], gs.at[4 + k], gr.at[4 + k], at_zl(k, 0))

    def group_y(k):
        return remote(gq.at[c, y], gq.at[c, y], gs.at[7 + k], gr.at[7 + k], at_y(k))

    group_c = remote(gq.at[c], gq.at[c], gs.at[0], gr.at[0], peer)

    nz[z] = jnp.sum((final * final).reshape(8, 8, 128), axis=0)
    for k in range(1, 8):
        tell_z(k).start()
        left.append(tell_z(k).wait_send)
    for k in range(1, 4):
        group_z(k).start()
        left.append(group_z(k).wait_send)
    for k in range(4):
        cross_z(k).start()
        left.append(cross_z(k).wait_send)
    for k in range(1, 8):
        tell_z(k).wait_recv()
    nxy[x * 4 + y] = jnp.sum(nz[...], axis=0)
    for k in range(15):
        tell_xy(k).start()
        left.append(tell_xy(k).wait_send)
    for k in range(1, 4):
        group_z(k).wait_recv()
    for k in range(1, 4):
        group_y(k).start()
        left.append(group_y(k).wait_send)
    for k in range(15):
        tell_xy(k).wait_recv()
    nc[c] = jnp.sum(nxy[...], axis=0)
    tell_c.start()
    left.append(tell_c.wait_send)
    for copy in state:
        copy.wait()
    for copy in lend:
        copy.wait_recv()
    for k in range(4):
        cross_z(k).wait_recv()
    tell_c.wait_recv()
    square = jnp.sum(nc[0] + nc[1], keepdims=True)
    factor = jnp.minimum(1.0, jnp.sqrt(F32(DW * KVW)) / jnp.sqrt(square + 1e-06))

    done = jnp.full((1, 128), steps[0].astype(F32))
    correct1 = 1.0 / (1.0 - jnp.exp(done * jnp.log(F32(0.9))))
    correct2 = 1.0 / (1.0 - jnp.exp(done * jnp.log(F32(0.95))))

    def adam(q, old, one, two):
        clipped = decoded(q, 0, 64, step_in(q, 64)) * factor
        one = 0.9 * one + 0.1 * clipped
        two = 0.95 * two + 0.05 * clipped * clipped
        new = old - 0.01 * ((one * correct1) / (jnp.sqrt(two * correct2) + 1e-08) + 0.1 * old)
        return clipped, new, one, two

    def half(sh):
        return span(sh * SH + c * HALF, HALF)

    def col(k):
        return span(((y + k + 4) % 4) * 128, 128)

    for n in range(4):
        rows = pl.ds(n * 64, 64)
        new = adam(oq.at[n], ow[0, rows, :], ow[1, rows, :], ow[2, rows, :])[1]
        params[span(other * SH + c * HALF + n * 64, 64), col(0)] = new.astype(BF16)

    def piece_x(sh, k, sem):
        ref = params.at[half(sh), col(0)]
        return remote(ref, ref, ps.at[sem], pr.at[sem], at_x(k))

    def piece_y(sh, k, sem):
        ref = params.at[half(sh), col(0)]
        return remote(ref, ref, ps.at[sem], pr.at[sem], at_y(k))

    @pl.when(c == 0)
    def _():
        for k in range(1, 4):
            piece_y(other, k, 11 + k).start()

    @pl.when(c == 1)
    def _():
        for k in range(1, 4):
            piece_x(other, k, 2 + k).start()

    def own_block(cc, yy, zz):
        rows = span(cc * HALF + zz * 64, 64)
        cols = span(yy * 128, 128)
        clipped, new, one, two = adam(gq.at[cc, yy, zz], w0[rows, cols], w1[rows, cols], w2[rows, cols])
        clipped_o[rows, cols] = clipped
        master_o[rows, cols] = new
        m1_o[rows, cols] = one
        m2_o[rows, cols] = two
        params[span(shard * SH + cc * HALF + zz * 64, 64), cols] = new.astype(BF16)

    @pl.loop(0, 4)
    def _(n):
        own_block(c, y, n)

    @pl.when(c == 1)
    def _():
        for k in range(1, 4):
            piece_x(shard, k, k - 1).start()

    for k in range(1, 4):
        group_y(k).wait_recv()
    group_c.start()
    left.append(group_c.wait_send)

    @pl.loop(0, 12)
    def _(n):
        own_block(c, (y + 1 + n // 4) % 4, n % 4)

    def near(e, k):
        return ((x + k + 4) % 4) * 2 + (1 - zh if e else zh)

    def to_peer(sh, sem):
        ref = params.at[half(sh), :]
        return remote(ref, ref, ks.at[sem], kr.at[sem], peer)

    def ring_x(e, n):
        owner, lower, way = ((0, 0, 1), (0, 1, 1), (0, 1, 3), (0, 0, 3), (-1, 0, 1), (1, 1, 3))[n]
        ref = params.at[span(near(e, owner) * SH + c * HALF + lower * 128, 128), :]
        return remote(ref, ref, ps.at[e * 6 + n], pr.at[e * 6 + n], at_x(way))

    def launch_x(e):
        for n in (0, 2, 1, 3):
            ring_x(e, n).start()

    def relay_x(e):
        ring_x(e, 0).wait_recv()
        ring_x(e, 4).start()
        ring_x(e, 2).wait_recv()
        ring_x(e, 5).start()

    def finish_x(e):
        ring_x(e, 1).wait_recv()
        to_peer(near(e, -1), e * 3 + 1).start()
        ring_x(e, 3).wait_recv()
        to_peer(near(e, 1), e * 3 + 2).start()
        ring_x(e, 4).wait_recv()
        ring_x(e, 5).wait_recv()
        to_peer(near(e, 2), e * 3 + 3).start()

    def ring_y(sh, n, m):
        owner, lower, rows, way = ((0, 0, 256, 1), (0, 0, 256, 3), (-1, 0, 128, 1), (1, 1, 128, 3))[m]
        ref = params.at[span(sh * SH + c * HALF + lower * 128, rows), col(owner)]
        return remote(ref, ref, ps.at[6 + n * 4 + m], pr.at[6 + n * 4 + m], at_y(way))

    order = [other] + [near(0, -k) for k in (1, 2, 3)] + [near(1, -k) for k in (1, 2, 3)]

    def launch_y(n):
        ring_y(order[n], n, 0).start()
        ring_y(order[n], n, 1).start()

    def relay_y(n):
        ring_y(order[n], n, 0).wait_recv()
        ring_y(order[n], n, 2).start()
        ring_y(order[n], n, 1).wait_recv()
        ring_y(order[n], n, 3).start()

    def rest():
        group_c.wait_recv()

        @pl.loop(0, 16)
        def _(n):
            own_block(1 - c, n // 4, n % 4)

    @pl.when(c == 0)
    def _():
        launch_x(0)
        rest()
        relay_x(0)
        for k in range(1, 4):
            piece_y(other, k, 11 + k).wait_recv()
        launch_x(1)
        to_peer(other, 0).start()
        finish_x(0)
        relay_x(1)
        finish_x(1)
        for n in range(6):
            ring_x(0, n).wait_send()
            ring_x(1, n).wait_send()
        for k in range(1, 4):
            piece_y(other, k, 11 + k).wait_send()

    @pl.when(c == 1)
    def _():
        launch_y(0)
        rest()
        for k in range(1, 4):
            piece_x(other, k, 2 + k).wait_recv()
            launch_y(3 + k)
        relay_y(0)
        for k in range(1, 4):
            piece_x(shard, k, k - 1).wait_recv()
            launch_y(k)
        for n in (4, 5, 6, 1, 2, 3):
            relay_y(n)
        for n in (0, 4, 5, 6, 1, 2, 3):
            ring_y(order[n], n, 2).wait_recv()
            ring_y(order[n], n, 3).wait_recv()
            to_peer(order[n], n).start()
        for k in range(1, 4):
            piece_x(shard, k, k - 1).wait_send()
            piece_x(other, k, 2 + k).wait_send()
        for n in range(7):
            for m in range(4):
                ring_y(order[n], n, m).wait_send()

    for n in range(7):
        to_peer(other, n).wait_recv()
        to_peer(other, n).wait_send()
    for wait in left:
        wait()


def store(*refs):
    copies = [pltpu.make_async_copy(refs[n], refs[5 + n], refs[10].at[n]) for n in range(5)]
    for copy in copies[::-1]:
        copy.start()
    for copy in copies:
        copy.wait()


def shards(activations, out_grad, master, moment_one, moment_two, alive, step_count):
    hbm = pl.BlockSpec(memory_space=pl.ANY)
    smem = pl.BlockSpec(memory_space=pltpu.SMEM)
    dma = pltpu.SemaphoreType.DMA
    vm = pltpu.VMEM
    results = [((SH, KVW), F32)] * 4 + [((DW, KVW), BF16)]
    held = pl.pallas_call(
        kernel,
        out_shape=[vm(*r) for r in results],
        in_specs=[hbm] * 5 + [smem] * 2,
        out_specs=[pl.BlockSpec(memory_space=vm)] * 5,
        scratch_shapes=[
            vm((TOK, DW), BF16), vm((TOK, KVW), BF16),
            vm((SH, KVW), F32), vm((SH, KVW), F32), vm((SH, KVW), F32), vm((3, HALF, 128), F32),
            vm((8, SH, KVW), F32), vm((8, HALF, KVW), F32),
            vm((8, QR, KVW), I16), vm((8, QR, KVW), I16), vm((24, QR, 128), I16),
            vm((2, QR, KVW), I16), vm((2, 3, QR, 128), I16), vm((2, 3, QR, 128), I16),
            vm((HALF, KVW), F32), vm((2, HALF, 128), F32),
            vm((8, 80, 128), I16), vm((8, 80, 128), I16),
            vm((64, 128), F32), vm((2, 4, 4, 80, 128), I16), vm((4, 80, 128), I16),
            vm((8, 8, 128), F32), vm((16, 8, 128), F32), vm((2, 8, 128), F32),
            dma((12,)), dma((8,)), dma((8,)), dma((24,)), dma((24,)), dma((6,)), dma((6,)), dma((8,)), dma((8,)),
            dma((3,)), dma((3,)), dma((23,)), dma((23,)), dma((11,)), dma((11,)), dma((34,)), dma((34,)),
            dma((7,)), dma((7,)),
        ],
        compiler_params=pltpu.CompilerParams(
            collective_id=0, has_side_effects=True, vmem_limit_bytes=50 * 2**20),
        name="reduce_update_gather",
    )(activations, out_grad, master, moment_one, moment_two, alive, step_count)
    return tuple(pl.pallas_call(
        store,
        out_shape=[jax.ShapeDtypeStruct(*r) for r in results],
        in_specs=[hbm] * 5,
        out_specs=[hbm] * 5,
        scratch_shapes=[dma((5,))],
        name="store_results",
    )(*held))


def solution(mesh):
    return jax.shard_map(
        shards,
        mesh=mesh,
        in_specs=(
            P(("replica", "shard"), None),
            P(("replica", "shard"), None),
            P("shard", None),
            P("shard", None),
            P("shard", None),
            P(),
            P(),
        ),
        out_specs=(P("shard", None), P("shard", None), P("shard", None), P("shard", None), P()),
        check_vma=False,
    )
```

```python
import functools

import jax
import jax.numpy as jnp
from jax import lax
from jax.experimental import pallas as pl
from jax.experimental.pallas import tpu as pltpu
from jax.sharding import PartitionSpec as P

DW = 4096
KVW = 512
TOK = 1024
SH = 512
HALF = 256
QR = HALF + 16
LEVELS = 32000.0
F32 = jnp.float32
BF16 = jnp.bfloat16
I16 = jnp.int16
MESH = pl.DeviceIdType.MESH


def place():
    r = lax.axis_index("replica")
    s = lax.axis_index("shard")
    return s // 2, r // 8, (s % 2) * 4 + (r // 2) % 4, r % 2


def dev(x, y, z, c):
    return ((y * 4 + z % 4) * 2 + c, x * 2 + z // 4)


def remote(src, dst, ssem, rsem, who):
    return pltpu.make_async_remote_copy(
        src_ref=src, dst_ref=dst, send_sem=ssem, recv_sem=rsem, device_id=who, device_id_type=MESH
    )


def span(start, size):
    return pl.ds(pl.multiple_of(start, size), size)


def step_of(code):
    return jnp.exp2(code * 0.125)


def fold_max(acc, block):
    rows, cols = block.shape
    return jnp.maximum(acc, jnp.max(jnp.abs(block).reshape(rows // 8, 8, cols), axis=0))


def code_of(largest):
    top = jnp.max(largest, axis=0, keepdims=True)
    code = jnp.clip(jnp.ceil(8.0 * jnp.log2(jnp.maximum(top, 1e-37) * (1.0 / LEVELS))), -960.0, 960.0)
    return code, step_of(-code)


def quantized(block, inverse):
    return jnp.round(block * inverse).astype(jnp.int32).astype(I16)


def code_rows(code):
    return jnp.broadcast_to(code.astype(jnp.int32), (16, code.shape[1])).astype(I16)


def encode(read, q, rows, cols, chunk, largest):
    code, inverse = code_of(largest)

    @pl.loop(0, rows // chunk, unroll=True)
    def _(i):
        at = pl.multiple_of(i * chunk, chunk)
        q[pl.ds(at, chunk), :] = quantized(read(at), inverse)

    q[pl.ds(rows, 16), :] = code_rows(code)


def step_in(q, rows):
    return step_of(q[pl.ds(rows, 16), :].astype(jnp.int32).astype(F32)[0:1, :])


def decoded(q, at, chunk, step):
    return q[pl.ds(at, chunk), :].astype(jnp.int32).astype(F32) * step


def kernel(act, grad, master, m1, m2, alive, steps, clipped_h, master_h, m1_h, m2_h, params,
           clipped_o, master_o, m1_o, m2_o, near_p, other_p, a, b, w0, w1, w2, ow, g, pq, got, own, q1s, q1rx, q1ry, q2x, q2y, q2r, full, part, q3s, q3r, block, gq, oq,
           nz, nxy, nc, asem, sent, cr, s1r, s2r, s3r, orr, nr, gr, pr, kr, local):
    x, y, z, c = place()
    zh, zl = z // 4, z % 4
    peer = dev(x, y, z, 1 - c)
    shard = x * 2 + zh
    other = x * 2 + 1 - zh
    left = []

    def at_x(k):
        return dev((x + k) % 4, y, z, c)

    def at_y(k):
        return dev(x, (y + k) % 4, z, c)

    def at_z(k):
        return dev(x, y, (z + k) % 8, c)

    def at_zl(k, h):
        return dev(x, y, (zh if h else 1 - zh) * 4 + (zl + k) % 4, c)

    xy = [(i, j) for i in range(4) for j in range(4) if (i, j) != (0, 0)]

    def at_xy(k):
        return dev((x + xy[k][0]) % 4, (y + xy[k][1]) % 4, z, c)

    barrier = pltpu.get_barrier_semaphore()
    pl.semaphore_signal(barrier, inc=1, device_id=peer, device_id_type=MESH)
    for k in range(15):
        pl.semaphore_signal(barrier, inc=1, device_id=at_xy(k), device_id_type=MESH)
    for k in range(1, 8):
        pl.semaphore_signal(barrier, inc=1, device_id=at_z(k), device_id_type=MESH)

    def a_copy(t):
        cols = span((((x + t % 4 + 1) % 4) * 2 + jnp.where(t < 4, 1 - zh, zh)) * SH, SH)
        return pltpu.make_async_copy(act.at[:, cols], a.at[:, cols], asem.at[t])

    b_copy = pltpu.make_async_copy(grad, b, asem.at[8])
    b_copy.start()
    for t in range(8):
        a_copy(t).start()
    state = [pltpu.make_async_copy(src, dst, asem.at[9 + n]) for n, (src, dst) in
             enumerate(((master, w0), (m1, w1), (m2, w2)))]
    for copy in state:
        copy.start()
    b_copy.wait()
    weight = alive[lax.axis_index("replica")].astype(F32)

    def core_copy(t):
        return remote(pq.at[t], got.at[t], sent.at[0], cr.at[t], peer)

    def wait_for(t):
        a_copy(t).wait()

    def product(t):
        cols = span((((x + t % 4 + 1) % 4) * 2 + jnp.where(t < 4, 1 - zh, zh)) * SH, SH)
        g[t] = lax.dot_general(a[:, cols], b[...], (((0,), (0,)), ((), ())), preferred_element_type=F32)

    def first_x(t):
        return remote(q1s.at[t], q1rx.at[t], sent.at[1], s1r.at[t], at_x(t % 4 + 1))

    def first_y(t, j):
        return remote(q1s.at[t, :, span(((y + j + 1) % 4) * 128, 128)], q1ry.at[t * 3 + j], sent.at[1],
                      s1r.at[t], at_y(j + 1))

    def for_peer(t):
        largest = jnp.zeros((8, KVW), F32)
        for n in range(8):
            largest = fold_max(largest, g[t, span((1 - c) * HALF + n * 32, 32), :])
        code, inverse = code_of(largest * weight)
        inverse = inverse * weight
        for n in range(8):
            pq[t, n * 32:(n + 1) * 32, :] = quantized(g[t, span((1 - c) * HALF + n * 32, 32), :], inverse)
        pq[t, HALF:QR, :] = code_rows(code)

    def summed(t):
        largest = jnp.zeros((8, KVW), F32)
        step = step_in(got.at[t], HALF)
        for n in range(8):
            rows = span(c * HALF + n * 32, 32)
            total = g[t, rows, :] * weight + decoded(got.at[t], n * 32, 32, step)
            own[t, n * 32:(n + 1) * 32, :] = total
            largest = fold_max(largest, total)
        return largest

    def coded(t, largest):
        code, inverse = code_of(largest)
        for n in range(8):
            q1s[t, n * 32:(n + 1) * 32, :] = quantized(own[t, n * 32:(n + 1) * 32, :], inverse)
        q1s[t, HALF:QR, :] = code_rows(code)

    def send(t):
        @pl.when(jnp.logical_and(c == 0, t % 4 < 3))
        def _():
            first_x(t).start()

        @pl.when(c == 1)
        def _():
            for j in range(3):
                first_y(t, j).start()

    for t in range(2):
        wait_for(t)
        product(t)
        for_peer(t)
        if t == 0:
            pl.semaphore_wait(barrier, 23)
        core_copy(t).start()
    piece = (span(c * HALF, HALF), span(y * 128, 128))
    lend = [remote(src.at[piece[0], piece[1]], ow.at[n], sent.at[2], orr.at[0], at_z(4)) for n, src in
            enumerate((master, m1, m2))]
    for copy in lend:
        copy.start()

    @pl.loop(2, 8)
    def _(t):
        wait_for(t)
        core_copy(t - 2).wait_recv()
        largest = summed(t - 2)
        product(t)
        coded(t - 2, largest)
        send(t - 2)
        for_peer(t)
        core_copy(t).start()

    @pl.loop(6, 8)
    def _(t):
        core_copy(t).wait_recv()
        coded(t, summed(t))
        send(t)

    def all_sent(sem, ref):
        left.append(remote(ref, ref, sent.at[sem], sent.at[sem], peer).wait_send)

    def came_all(ref, sem):
        remote(ref, ref, sent.at[0], sem, peer).wait_recv()

    all_sent(0, pq)
    all_sent(1, q1s.at[0:6])
    all_sent(2, ow)

    def second_y(h, j):
        return remote(q2x.at[h, :, span(((y + j + 1) % 4) * 128, 128)], q2r.at[h, j], sent.at[3],
                      s2r.at[h], at_y(j + 1))

    def second_x(h, i):
        return remote(q2y.at[h, i], q2r.at[h, i], sent.at[3], s2r.at[h], at_x(i + 1))

    def first_sums(h):
        @pl.when(c == 0)
        def _():
            for i in range(3):
                first_x(h * 4 + i).wait_recv()
            step = [step_in(q1rx.at[h * 4 + i], HALF) for i in range(3)]

            def add(n, acc):
                at = pl.multiple_of(n * 32, 32)
                total = own[h * 4 + 3, pl.ds(at, 32), :]
                for i in range(3):
                    total += decoded(q1rx.at[h * 4 + i], at, 32, step[i])
                full[pl.ds(at, 32), :] = total
                return fold_max(acc, total)

            largest = lax.fori_loop(0, HALF // 32, add, jnp.zeros((8, KVW), F32))
            encode(lambda at: full[pl.ds(at, 32), :], q2x.at[h], HALF, KVW, 32, largest)
            for j in range(3):
                second_y(h, j).start()
            part[h] = full[:, span(y * 128, 128)]

        @pl.when(c == 1)
        def _():
            @pl.loop(0, 4)
            def _(i):
                t = h * 4 + i
                came_all(q1ry.at[pl.ds(t * 3, 3)], s1r.at[t])
                step = [step_in(q1ry.at[t * 3 + j], HALF) for j in range(3)]

                def add(n, acc):
                    at = pl.multiple_of(n * 128, 128)
                    total = own[t, pl.ds(at, 128), span(y * 128, 128)]
                    for j in range(3):
                        total += decoded(q1ry.at[t * 3 + j], at, 128, step[j])
                    part[h, pl.ds(at, 128), :] = total
                    return fold_max(acc, total)

                largest = lax.fori_loop(0, 2, add, jnp.zeros((8, 128), F32))

                @pl.when(i < 3)
                def _():
                    encode(lambda at: part[h, pl.ds(at, 128), :], q2y.at[h, i], HALF, 128, 128, largest)
                    second_x(h, i).start()

    def third(h, k):
        n = h * 3 + k
        return remote(q3s.at[n], q3r.at[n], sent.at[4], s3r.at[0], at_zl(k, h))

    def second_sums(h):
        came_all(q2r.at[h], s2r.at[h])
        step = [step_in(q2r.at[h, j], HALF) for j in range(3)]
        largest = jnp.zeros((8, 128), F32)
        for n in range(4):
            at = n * 64
            total = part[h, at:at + 64, :]
            for j in range(3):
                total += decoded(q2r.at[h, j], at, 64, step[j])
            part[h, at:at + 64, :] = total
            largest = fold_max(largest, total)
        code, inverse = code_of(largest)
        for k in range(h, 4):
            q3s[h * 3 + k, 0:64, :] = quantized(part[h, span(((zl + k) % 4) * 64, 64), :], inverse)
            q3s[h * 3 + k, 64:80, :] = code_rows(code)
        for k in range(h, 4):
            third(h, k).start()

    all_sent(3, q2r)
    all_sent(4, q3s)
    first_sums(0)
    second_sums(0)
    first_sums(1)
    second_sums(1)
    total = part[1, span(zl * 64, 64), :]
    came_all(q3r, s3r.at[0])
    for n in range(7):
        total += decoded(q3r.at[n], 0, 64, step_in(q3r.at[n], 64))

    mine = gq.at[c, y, zl]
    def tell_z(k):
        return remote(nz.at[z], nz.at[z], sent.at[5], nr.at[0], at_z(k))

    def tell_xy(k):
        slot = nxy.at[x * 4 + y]
        return remote(slot, slot, sent.at[6], nr.at[1], at_xy(k))

    tell_c = remote(nc.at[c], nc.at[c], sent.at[7], nr.at[2], peer)

    def group_z(k):
        return remote(mine, mine, sent.at[8], gr.at[0], at_zl(k, 1))

    def cross_z(k):
        return remote(mine, oq.at[zl], sent.at[9], gr.at[1], at_zl(k, 0))

    def group_y(k):
        return remote(gq.at[c, y], gq.at[c, y], sent.at[10], gr.at[2], at_y(k))

    group_c = remote(gq.at[c], gq.at[c], sent.at[11], gr.at[3], peer)

    nz[z] = jnp.sum((total * total).reshape(8, 8, 128), axis=0)
    for k in range(1, 8):
        tell_z(k).start()
    encode(lambda at: total, mine, 64, 128, 64, fold_max(jnp.zeros((8, 128), F32), total))
    for k in range(1, 4):
        group_z(k).start()
    came_all(nz.at[0:7], nr.at[0])
    nxy[x * 4 + y] = jnp.sum(nz[...], axis=0)
    for k in range(15):
        tell_xy(k).start()
    for k in range(4):
        cross_z(k).start()
    came_all(gq.at[0, 0, 0:3], gr.at[0])
    for k in range(1, 4):
        group_y(k).start()
    came_all(nxy.at[0:15], nr.at[1])
    nc[c] = jnp.sum(nxy[...], axis=0)
    tell_c.start()
    for copy in state:
        copy.wait()
    came_all(ow, orr.at[0])
    came_all(oq, gr.at[1])
    tell_c.wait_recv()
    square = jnp.sum(nc[0] + nc[1], keepdims=True)
    factor = jnp.minimum(1.0, jnp.sqrt(F32(DW * KVW)) / jnp.sqrt(square + 1e-06))

    all_sent(5, nz.at[0:7])
    all_sent(6, nxy.at[0:15])
    all_sent(7, nc.at[0])
    all_sent(8, gq.at[0, 0, 0:3])
    all_sent(9, oq)
    all_sent(10, gq.at[0, 0:3])

    done = jnp.full((1, 128), steps[0].astype(F32))
    correct1 = 1.0 / (1.0 - jnp.exp(done * jnp.log(F32(0.9))))
    correct2 = 1.0 / (1.0 - jnp.exp(done * jnp.log(F32(0.95))))

    def adam(q, old, one, two):
        clipped = decoded(q, 0, 64, step_in(q, 64)) * factor
        one = 0.9 * one + 0.1 * clipped
        two = 0.95 * two + 0.05 * clipped * clipped
        new = old - 0.01 * ((one * correct1) / (jnp.sqrt(two * correct2) + 1e-08) + 0.1 * old)
        return clipped, new, one, two

    def half(sh):
        return span(sh * SH + c * HALF, HALF)

    def col(k):
        return span(((y + k + 4) % 4) * 128, 128)

    for n in range(4):
        rows = pl.ds(n * 64, 64)
        new = adam(oq.at[n], ow[0, rows, :], ow[1, rows, :], ow[2, rows, :])[1]
        other_p[n * 64:(n + 1) * 64, :] = new.astype(BF16)

    rows_c = span(c * HALF, HALF)

    def piece_x(e, k):
        src = other_p if e else near_p.at[rows_c, col(0)]
        return remote(src, params.at[half(other if e else shard), col(0)], sent.at[12], pr.at[e * 3 + k - 1], at_x(k))

    def piece_y(k):
        return remote(other_p, params.at[half(other), col(0)], sent.at[12], pr.at[12], at_y(k))

    keep_other = pltpu.make_async_copy(other_p, params.at[half(other), col(0)], local.at[0])
    keep_other.start()

    @pl.when(c == 0)
    def _():
        for k in range(1, 4):
            piece_y(k).start()

    @pl.when(c == 1)
    def _():
        for k in range(1, 4):
            piece_x(1, k).start()

    def own_block(cc, yy, zz):
        rows = span(cc * HALF + zz * 64, 64)
        cols = span(yy * 128, 128)
        clipped, new, one, two = adam(gq.at[cc, yy, zz], w0[rows, cols], w1[rows, cols], w2[rows, cols])
        clipped_o[rows, cols] = clipped
        master_o[rows, cols] = new
        m1_o[rows, cols] = one
        m2_o[rows, cols] = two
        near_p[rows, cols] = new.astype(BF16)

    for n in range(4):
        own_block(c, y, n)

    @pl.when(c == 1)
    def _():
        for k in range(1, 4):
            piece_x(0, k).start()

    came_all(gq.at[0, 0:3], gr.at[2])
    group_c.start()
    all_sent(11, gq.at[0])

    @pl.loop(0, 12, unroll=4)
    def _(n):
        own_block(c, (y + 1 + n // 4) % 4, n % 4)

    def near(e, k):
        return ((x + k + 4) % 4) * 2 + (1 - zh if e else zh)

    def to_peer(sh):
        ref = params.at[half(sh), :]
        return remote(ref, ref, sent.at[13], kr.at[0], peer)

    def ring_x(e, n):
        owner, lower, way = ((0, 0, 1), (0, 1, 1), (0, 1, 3), (0, 0, 3), (-1, 0, 1), (1, 1, 3))[n]
        ref = params.at[span(near(e, owner) * SH + c * HALF + lower * 128, 128), :]
        src = near_p.at[span(c * HALF + lower * 128, 128), :] if e == 0 and n < 4 else ref
        return remote(src, ref, sent.at[12], pr.at[e * 6 + n], at_x(way))

    def launch_x(e):
        for n in (0, 2, 1, 3):
            ring_x(e, n).start()

    def relay_x(e):
        ring_x(e, 0).wait_recv()
        ring_x(e, 4).start()
        ring_x(e, 2).wait_recv()
        ring_x(e, 5).start()

    def finish_x(e):
        ring_x(e, 1).wait_recv()
        to_peer(near(e, -1)).start()
        ring_x(e, 3).wait_recv()
        to_peer(near(e, 1)).start()
        ring_x(e, 4).wait_recv()
        ring_x(e, 5).wait_recv()
        to_peer(near(e, 2)).start()

    def ring_y(sh, n, m):
        owner, lower, rows, way = ((0, 0, 256, 1), (0, 0, 256, 3), (-1, 0, 128, 1), (1, 1, 128, 3))[m]
        ref = params.at[span(sh * SH + c * HALF + lower * 128, rows), col(owner)]
        src = other_p if n == 0 and m < 2 else ref
        return remote(src, ref, sent.at[12], pr.at[6 + n * 3 + min(m, 2)], at_y(way))

    order = [other] + [near(0, -k) for k in (1, 2, 3)] + [near(1, -k) for k in (1, 2, 3)]

    def launch_y(n):
        ring_y(order[n], n, 0).start()
        ring_y(order[n], n, 1).start()

    def relay_y(n):
        ring_y(order[n], n, 0).wait_recv()
        ring_y(order[n], n, 2).start()
        ring_y(order[n], n, 1).wait_recv()
        ring_y(order[n], n, 3).start()

    outs = [(clipped_o, clipped_h), (master_o, master_h), (m1_o, m1_h), (m2_o, m2_h), (near_p, params.at[span(shard * SH, SH), :])]
    keep = [pltpu.make_async_copy(src, dst, local.at[1 + n]) for n, (src, dst) in enumerate(outs)]

    def rest():
        group_c.wait_recv()

        @pl.loop(0, 16, unroll=4)
        def _(n):
            own_block(1 - c, n // 4, n % 4)

        for copy in keep:
            copy.start()
        keep_other.wait()

    @pl.when(c == 0)
    def _():
        launch_x(0)
        rest()
        relay_x(0)
        came_all(params.at[half(other), 0:384], pr.at[12])
        launch_x(1)
        to_peer(other).start()
        finish_x(0)
        relay_x(1)
        finish_x(1)

    @pl.when(c == 1)
    def _():
        launch_y(0)
        rest()
        for k in range(1, 4):
            piece_x(1, k).wait_recv()
            launch_y(3 + k)
        relay_y(0)
        for k in range(1, 4):
            piece_x(0, k).wait_recv()
            launch_y(k)
        for n in (4, 5, 6, 1, 2, 3):
            relay_y(n)
        for n in (0, 4, 5, 6, 1, 2, 3):
            came_all(params.at[half(order[n]), 0:128], pr.at[6 + n * 3 + 2])
            to_peer(order[n]).start()
    came_all(params.at[0:7 * HALF, :], kr.at[0])
    all_sent(12, params.at[0:27 * 64, :])
    all_sent(13, params.at[0:7 * HALF, :])
    for copy in keep:
        copy.wait()
    for wait in left:
        wait()


def store(*refs):
    copies = [pltpu.make_async_copy(refs[n], refs[5 + n], refs[10].at[n]) for n in range(5)]
    for copy in copies[::-1]:
        copy.start()
    for copy in copies:
        copy.wait()


def shards(activations, out_grad, master, moment_one, moment_two, alive, step_count):
    hbm = pl.BlockSpec(memory_space=pl.ANY)
    dma = pltpu.SemaphoreType.DMA
    vm = pltpu.VMEM
    results = [((SH, KVW), F32)] * 4 + [((DW, KVW), BF16)]
    held = pl.pallas_call(
        kernel,
        out_shape=[vm(*r) for r in results],
        in_specs=[hbm] * 5 + [pl.BlockSpec(memory_space=pltpu.SMEM)] * 2,
        out_specs=[hbm] * 5,
        scratch_shapes=[
            vm((SH, KVW), F32), vm((SH, KVW), F32), vm((SH, KVW), F32), vm((SH, KVW), F32),
            vm((SH, KVW), BF16), vm((HALF, 128), BF16),
            vm((TOK, DW), BF16), vm((TOK, KVW), BF16),
            vm((SH, KVW), F32), vm((SH, KVW), F32), vm((SH, KVW), F32), vm((3, HALF, 128), F32),
            vm((8, SH, KVW), F32), vm((8, QR, KVW), I16), vm((8, QR, KVW), I16), vm((8, HALF, KVW), F32),
            vm((8, QR, KVW), I16), vm((8, QR, KVW), I16), vm((24, QR, 128), I16),
            vm((2, QR, KVW), I16), vm((2, 3, QR, 128), I16), vm((2, 3, QR, 128), I16),
            vm((HALF, KVW), F32), vm((2, HALF, 128), F32),
            vm((7, 80, 128), I16), vm((7, 80, 128), I16),
            vm((64, 128), F32), vm((2, 4, 4, 80, 128), I16), vm((4, 80, 128), I16),
            vm((8, 8, 128), F32), vm((16, 8, 128), F32), vm((2, 8, 128), F32),
            dma((12,)), dma((14,)), dma((8,)), dma((8,)), dma((2,)), dma((1,)), dma((1,)), dma((3,)), dma((4,)),
            dma((27,)), dma((1,)), dma((6,)),
        ],
        compiler_params=pltpu.CompilerParams(
            collective_id=0, has_side_effects=True, vmem_limit_bytes=50 * 2**20),
        name="reduce_update_gather",
    )(activations, out_grad, master, moment_one, moment_two, alive, step_count)
    return tuple(pl.pallas_call(
        store,
        out_shape=[jax.ShapeDtypeStruct(*r) for r in results],
        in_specs=[hbm] * 5,
        out_specs=[hbm] * 5,
        scratch_shapes=[dma((5,))],
        compiler_params=pltpu.CompilerParams(vmem_limit_bytes=2**20),
        name="store_results",
    )(*(pltpu.with_memory_space_constraint(v, vm) for v in held)))


def solution(mesh):
    return jax.shard_map(
        shards,
        mesh=mesh,
        in_specs=(
            P(("replica", "shard"), None),
            P(("replica", "shard"), None),
            P("shard", None),
            P("shard", None),
            P("shard", None),
            P(),
            P(),
        ),
        out_specs=(P("shard", None), P("shard", None), P("shard", None), P("shard", None), P()),
        check_vma=False,
    )
```

```python
import functools

import jax
import jax.numpy as jnp
from jax import lax
from jax.experimental import pallas as pl
from jax.experimental.pallas import tpu as pltpu
from jax.sharding import PartitionSpec as P

DW = 4096
KVW = 512
TOK = 1024
SH = 512
HALF = 256
QR = HALF + 16
LEVELS = 32000.0
F32 = jnp.float32
BF16 = jnp.bfloat16
I16 = jnp.int16
MESH = pl.DeviceIdType.MESH


def place():
    r = lax.axis_index("replica")
    s = lax.axis_index("shard")
    return s // 2, r // 8, (s % 2) * 4 + (r // 2) % 4, r % 2


def dev(x, y, z, c):
    return ((y * 4 + z % 4) * 2 + c, x * 2 + z // 4)


def remote(src, dst, ssem, rsem, who):
    return pltpu.make_async_remote_copy(
        src_ref=src, dst_ref=dst, send_sem=ssem, recv_sem=rsem, device_id=who, device_id_type=MESH
    )


def span(start, size):
    return pl.ds(pl.multiple_of(start, size), size)


def step_of(code):
    return jnp.exp2(code * 0.125)


def fold_max(acc, block):
    rows, cols = block.shape
    return jnp.maximum(acc, jnp.max(jnp.abs(block).reshape(rows // 8, 8, cols), axis=0))


def code_of(largest):
    top = jnp.max(largest, axis=0, keepdims=True)
    code = jnp.clip(jnp.ceil(8.0 * jnp.log2(jnp.maximum(top, 1e-37) * (1.0 / LEVELS))), -960.0, 960.0)
    return code, step_of(-code)


def quantized(block, inverse):
    return jnp.round(block * inverse).astype(jnp.int32).astype(I16)


def code_rows(code):
    return jnp.broadcast_to(code.astype(jnp.int32), (16, code.shape[1])).astype(I16)


def encode(read, q, rows, cols, chunk, largest):
    code, inverse = code_of(largest)

    @pl.loop(0, rows // chunk, unroll=True)
    def _(i):
        at = pl.multiple_of(i * chunk, chunk)
        q[pl.ds(at, chunk), :] = quantized(read(at), inverse)

    q[pl.ds(rows, 16), :] = code_rows(code)


def step_in(q, rows):
    return step_of(q[pl.ds(rows, 16), :].astype(jnp.int32).astype(F32)[0:1, :])


def decoded(q, at, chunk, step):
    return q[pl.ds(at, chunk), :].astype(jnp.int32).astype(F32) * step


def kernel(act, grad, master, m1, m2, alive, steps, clipped_h, master_h, m1_h, m2_h, params,
           clipped_o, master_o, m1_o, m2_o, near_p, other_p, a, b, w0, w1, w2, ow, g, pq, got, own, q1s, q1rx, q1ry, q2x, q2y, q2r, full, part, q3s, q3r, block, gq, oq,
           nz, nxy, nc, asem, sent, cr, s1r, s2r, s3r, orr, nr, gr, pr, kr, local):
    x, y, z, c = place()
    zh, zl = z // 4, z % 4
    peer = dev(x, y, z, 1 - c)
    shard = x * 2 + zh
    other = x * 2 + 1 - zh
    left = []

    def at_x(k):
        return dev((x + k) % 4, y, z, c)

    def at_y(k):
        return dev(x, (y + k) % 4, z, c)

    def at_z(k):
        return dev(x, y, (z + k) % 8, c)

    def at_zl(k, h):
        return dev(x, y, (zh if h else 1 - zh) * 4 + (zl + k) % 4, c)

    xy = [(i, j) for i in range(4) for j in range(4) if (i, j) != (0, 0)]

    def at_xy(k):
        return dev((x + xy[k][0]) % 4, (y + xy[k][1]) % 4, z, c)

    barrier = pltpu.get_barrier_semaphore()
    pl.semaphore_signal(barrier, inc=1, device_id=peer, device_id_type=MESH)
    for k in range(15):
        pl.semaphore_signal(barrier, inc=1, device_id=at_xy(k), device_id_type=MESH)
    for k in range(1, 8):
        pl.semaphore_signal(barrier, inc=1, device_id=at_z(k), device_id_type=MESH)

    def a_copy(t):
        cols = span((((x + t % 4 + 1) % 4) * 2 + jnp.where(t < 4, 1 - zh, zh)) * SH, SH)
        return pltpu.make_async_copy(act.at[:, cols], a.at[:, cols], asem.at[t])

    b_copy = pltpu.make_async_copy(grad, b, asem.at[8])
    b_copy.start()
    for t in range(8):
        a_copy(t).start()
    state = [pltpu.make_async_copy(src, dst, asem.at[9 + n]) for n, (src, dst) in
             enumerate(((master, w0), (m1, w1), (m2, w2)))]
    for copy in state:
        copy.start()
    b_copy.wait()
    weight = alive[lax.axis_index("replica")].astype(F32)

    def core_copy(t):
        return remote(pq.at[t], got.at[t], sent.at[0], cr.at[t], peer)

    def wait_for(t):
        a_copy(t).wait()

    def product(t):
        cols = span((((x + t % 4 + 1) % 4) * 2 + jnp.where(t < 4, 1 - zh, zh)) * SH, SH)
        g[t] = lax.dot_general(a[:, cols], b[...], (((0,), (0,)), ((), ())), preferred_element_type=F32)

    def first_x(t):
        return remote(q1s.at[t], q1rx.at[t], sent.at[1], s1r.at[t], at_x(t % 4 + 1))

    def first_y(t, j):
        return remote(q1s.at[t, :, span(((y + j + 1) % 4) * 128, 128)], q1ry.at[t * 3 + j], sent.at[1],
                      s1r.at[t], at_y(j + 1))

    def for_peer(t):
        largest = jnp.zeros((8, KVW), F32)
        for n in range(8):
            largest = fold_max(largest, g[t, span((1 - c) * HALF + n * 32, 32), :])
        code, inverse = code_of(largest * weight)
        inverse = inverse * weight
        for n in range(8):
            pq[t, n * 32:(n + 1) * 32, :] = quantized(g[t, span((1 - c) * HALF + n * 32, 32), :], inverse)
        pq[t, HALF:QR, :] = code_rows(code)

    def summed(t):
        largest = jnp.zeros((8, KVW), F32)
        step = step_in(got.at[t], HALF)
        for n in range(8):
            rows = span(c * HALF + n * 32, 32)
            total = g[t, rows, :] * weight + decoded(got.at[t], n * 32, 32, step)
            own[t, n * 32:(n + 1) * 32, :] = total
            largest = fold_max(largest, total)
        return largest

    def coded(t, largest):
        code, inverse = code_of(largest)
        for n in range(8):
            q1s[t, n * 32:(n + 1) * 32, :] = quantized(own[t, n * 32:(n + 1) * 32, :], inverse)
        q1s[t, HALF:QR, :] = code_rows(code)

    def send(t):
        @pl.when(jnp.logical_and(c == 0, t % 4 < 3))
        def _():
            first_x(t).start()

        @pl.when(c == 1)
        def _():
            for j in range(3):
                first_y(t, j).start()

    for t in range(2):
        wait_for(t)
        product(t)
        for_peer(t)
        if t == 0:
            pl.semaphore_wait(barrier, 23)
        core_copy(t).start()
    piece = (span(c * HALF, HALF), span(y * 128, 128))
    lend = [remote(src.at[piece[0], piece[1]], ow.at[n], sent.at[2], orr.at[0], at_z(4)) for n, src in
            enumerate((master, m1, m2))]
    for copy in lend:
        copy.start()

    @pl.loop(2, 8)
    def _(t):
        wait_for(t)
        core_copy(t - 2).wait_recv()
        largest = summed(t - 2)
        product(t)
        coded(t - 2, largest)
        send(t - 2)
        for_peer(t)
        core_copy(t).start()

    @pl.loop(6, 8)
    def _(t):
        core_copy(t).wait_recv()
        coded(t, summed(t))
        send(t)

    def all_sent(sem, ref):
        left.append(remote(ref, ref, sent.at[sem], sent.at[sem], peer).wait_send)

    def came_all(ref, sem):
        remote(ref, ref, sent.at[0], sem, peer).wait_recv()

    all_sent(0, pq)
    all_sent(1, q1s.at[0:6])
    all_sent(2, ow)

    def second_y(h, j):
        return remote(q2x.at[h, :, span(((y + j + 1) % 4) * 128, 128)], q2r.at[h, j], sent.at[3],
                      s2r.at[h], at_y(j + 1))

    def second_x(h, i):
        return remote(q2y.at[h, i], q2r.at[h, i], sent.at[3], s2r.at[h], at_x(i + 1))

    def first_sums(h):
        @pl.when(c == 0)
        def _():
            for i in range(3):
                first_x(h * 4 + i).wait_recv()
            step = [step_in(q1rx.at[h * 4 + i], HALF) for i in range(3)]

            def add(n, acc):
                at = pl.multiple_of(n * 32, 32)
                total = own[h * 4 + 3, pl.ds(at, 32), :]
                for i in range(3):
                    total += decoded(q1rx.at[h * 4 + i], at, 32, step[i])
                full[pl.ds(at, 32), :] = total
                return fold_max(acc, total)

            largest = lax.fori_loop(0, HALF // 32, add, jnp.zeros((8, KVW), F32))
            encode(lambda at: full[pl.ds(at, 32), :], q2x.at[h], HALF, KVW, 32, largest)
            for j in range(3):
                second_y(h, j).start()
            part[h] = full[:, span(y * 128, 128)]

        @pl.when(c == 1)
        def _():
            @pl.loop(0, 4)
            def _(i):
                t = h * 4 + i
                came_all(q1ry.at[pl.ds(t * 3, 3)], s1r.at[t])
                step = [step_in(q1ry.at[t * 3 + j], HALF) for j in range(3)]

                def add(n, acc):
                    at = pl.multiple_of(n * 128, 128)
                    total = own[t, pl.ds(at, 128), span(y * 128, 128)]
                    for j in range(3):
                        total += decoded(q1ry.at[t * 3 + j], at, 128, step[j])
                    part[h, pl.ds(at, 128), :] = total
                    return fold_max(acc, total)

                largest = lax.fori_loop(0, 2, add, jnp.zeros((8, 128), F32))

                @pl.when(i < 3)
                def _():
                    encode(lambda at: part[h, pl.ds(at, 128), :], q2y.at[h, i], HALF, 128, 128, largest)
                    second_x(h, i).start()

    def third(h, k):
        n = h * 3 + k
        return remote(q3s.at[n], q3r.at[n], sent.at[4], s3r.at[0], at_zl(k, h))

    def second_sums(h):
        came_all(q2r.at[h], s2r.at[h])
        step = [step_in(q2r.at[h, j], HALF) for j in range(3)]
        largest = jnp.zeros((8, 128), F32)
        for n in range(4):
            at = n * 64
            total = part[h, at:at + 64, :]
            for j in range(3):
                total += decoded(q2r.at[h, j], at, 64, step[j])
            part[h, at:at + 64, :] = total
            largest = fold_max(largest, total)
        code, inverse = code_of(largest)
        for k in range(h, 4):
            q3s[h * 3 + k, 0:64, :] = quantized(part[h, span(((zl + k) % 4) * 64, 64), :], inverse)
            q3s[h * 3 + k, 64:80, :] = code_rows(code)
        for k in range(h, 4):
            third(h, k).start()

    all_sent(3, q2r)
    all_sent(4, q3s)
    first_sums(0)
    second_sums(0)
    first_sums(1)
    second_sums(1)
    total = part[1, span(zl * 64, 64), :]
    came_all(q3r, s3r.at[0])
    for n in range(7):
        total += decoded(q3r.at[n], 0, 64, step_in(q3r.at[n], 64))

    mine = gq.at[c, y, zl]
    def tell_z(k):
        return remote(nz.at[z], nz.at[z], sent.at[5], nr.at[0], at_z(k))

    def tell_xy(k):
        slot = nxy.at[x * 4 + y]
        return remote(slot, slot, sent.at[6], nr.at[1], at_xy(k))

    tell_c = remote(nc.at[c], nc.at[c], sent.at[7], nr.at[2], peer)

    def group_z(k):
        return remote(mine, mine, sent.at[8], gr.at[0], at_zl(k, 1))

    def cross_z(k):
        return remote(mine, oq.at[zl], sent.at[9], gr.at[1], at_zl(k, 0))

    def group_y(k):
        return remote(gq.at[c, y], gq.at[c, y], sent.at[10], gr.at[2], at_y(k))

    group_c = remote(gq.at[c], gq.at[c], sent.at[11], gr.at[3], peer)

    nz[z] = jnp.sum((total * total).reshape(8, 8, 128), axis=0)
    for k in range(1, 8):
        tell_z(k).start()
    encode(lambda at: total, mine, 64, 128, 64, fold_max(jnp.zeros((8, 128), F32), total))
    for k in range(1, 4):
        group_z(k).start()
    for k in range(4):
        cross_z(k).start()
    came_all(nz.at[0:7], nr.at[0])
    nxy[x * 4 + y] = jnp.sum(nz[...], axis=0)
    for k in range(15):
        tell_xy(k).start()
    came_all(gq.at[0, 0, 0:3], gr.at[0])

    @pl.when(c == 0)
    def _():
        for k in range(1, 4):
            group_y(k).start()

    came_all(nxy.at[0:15], nr.at[1])
    nc[c] = jnp.sum(nxy[...], axis=0)
    tell_c.start()
    for copy in state:
        copy.wait()
    came_all(ow, orr.at[0])
    came_all(oq, gr.at[1])
    tell_c.wait_recv()
    square = jnp.sum(nc[0] + nc[1], keepdims=True)
    factor = jnp.minimum(1.0, jnp.sqrt(F32(DW * KVW)) / jnp.sqrt(square + 1e-06))

    all_sent(5, nz.at[0:7])
    all_sent(6, nxy.at[0:15])
    all_sent(7, nc.at[0])
    all_sent(8, gq.at[0, 0, 0:3])
    all_sent(9, oq)
    all_sent(10, gq.at[0, 0:3])

    done = jnp.full((1, 128), steps[0].astype(F32))
    correct1 = 1.0 / (1.0 - jnp.exp(done * jnp.log(F32(0.9))))
    correct2 = 1.0 / (1.0 - jnp.exp(done * jnp.log(F32(0.95))))

    def adam(q, old, one, two):
        clipped = decoded(q, 0, 64, step_in(q, 64)) * factor
        one = 0.9 * one + 0.1 * clipped
        two = 0.95 * two + 0.05 * clipped * clipped
        new = old - 0.01 * ((one * correct1) / (jnp.sqrt(two * correct2) + 1e-08) + 0.1 * old)
        return clipped, new, one, two

    def col(k):
        return span(((y + k + 4) % 4) * 128, 128)

    for n in range(4):
        rows = pl.ds(n * 64, 64)
        new = adam(oq.at[n], ow[0, rows, :], ow[1, rows, :], ow[2, rows, :])[1]
        other_p[n * 64:(n + 1) * 64, :] = new.astype(BF16)

    rows_c = span(c * HALF, HALF)

    def own_block(cc, yy, zz):
        rows = span(cc * HALF + zz * 64, 64)
        cols = span(yy * 128, 128)
        clipped, new, one, two = adam(gq.at[cc, yy, zz], w0[rows, cols], w1[rows, cols], w2[rows, cols])
        clipped_o[rows, cols] = clipped
        master_o[rows, cols] = new
        m1_o[rows, cols] = one
        m2_o[rows, cols] = two
        near_p[rows, cols] = new.astype(BF16)

    def other_blocks():
        @pl.loop(0, 12, unroll=4)
        def _(n):
            own_block(c, (y + 1 + n // 4) % 4, n % 4)

    outs = [(clipped_o, clipped_h), (master_o, master_h), (m1_o, m1_h), (m2_o, m2_h)]

    def keep(cc, n):
        rows = span(cc * HALF, HALF)
        copies = [pltpu.make_async_copy(src.at[rows, :], dst.at[rows, :], local.at[n + i]) for i, (src, dst) in enumerate(outs)]
        there = params.at[span(shard * SH + cc * HALF, HALF), :]
        return copies + [pltpu.make_async_copy(near_p.at[rows, :], there, local.at[n + 4])]

    def rest():
        group_c.wait_recv()

        @pl.loop(0, 16, unroll=4)
        def _(n):
            own_block(1 - c, n // 4, n % 4)

        for copy in keep(1 - c, 6):
            copy.start()

    def near(e, k):
        return ((x + k + 4) % 4) * 2 + (1 - zh if e else zh)

    def some(sh, first, rows):
        return pl.ds(pl.multiple_of(sh * SH + c * HALF + first, 64), rows)

    def to_peer(sh, first, rows):
        ref = params.at[some(sh, first, rows), :]
        remote(ref, ref, sent.at[13], kr.at[0], peer).start()

    def gather(src, dst, sem, who):
        return remote(src, dst, sent.at[12], pr.at[sem], who)

    def piece_x(e, k, first, rows, sem):
        src = other_p.at[first:first + rows, :] if e else near_p.at[some(0, first, rows), col(0)]
        return gather(src, params.at[some(near(e, 0), first, rows), col(0)], sem + k - 1, at_x(k))

    def piece_y(k):
        return gather(other_p.at[0:128, :], params.at[some(other, 0, 128), col(0)], 12, at_y(k))

    def ring_x(e, n):
        owner, lower, way = ((0, 0, 1), (0, 1, 1), (0, 1, 3), (0, 0, 3), (-1, 0, 1), (1, 1, 3))[n]
        rows = 64 if e else 128
        ref = params.at[some(near(e, owner), lower * rows, rows), :]
        src = near_p.at[some(0, lower * rows, rows), :] if e == 0 and n < 4 else ref
        return gather(src, ref, e * 6 + n, at_x(way))

    def launch_x(e):
        for n in (0, 2, 1, 3):
            ring_x(e, n).start()

    def relay_x(e):
        rows = 64 if e else 128
        ring_x(e, 0).wait_recv()
        ring_x(e, 4).start()
        ring_x(e, 2).wait_recv()
        ring_x(e, 5).start()
        to_peer(near(e, -1), 0, rows)
        to_peer(near(e, 1), rows, rows)

    def finish_x(e):
        rows = 64 if e else 128
        for n, owner, lower in ((1, -1, 1), (3, 1, 0), (4, 2, 0), (5, 2, 1)):
            ring_x(e, n).wait_recv()
            to_peer(near(e, owner), lower * rows, rows)

    class RingY:
        def __init__(self, sh, src, first, rows, sem):
            self.sh, self.src, self.first, self.rows, self.sem = sh, src, first, rows, sem

        def copy(self, m):
            owner, lower, part, way = ((0, 0, 1, 1), (0, 0, 1, 3), (-1, 0, 2, 1), (1, 1, 2, 3))[m]
            size = self.rows // part
            ref = params.at[some(self.sh, self.first + lower * size, size), col(owner)]
            src = self.src if self.src is not None and m < 2 else ref
            return gather(src, ref, self.sem + min(m, 2), at_y(way))

        def launch(self):
            self.copy(0).start()
            self.copy(1).start()

        def relay(self):
            self.copy(0).wait_recv()
            self.copy(2).start()
            self.copy(1).wait_recv()
            self.copy(3).start()

        def finish(self):
            came_all(params.at[some(self.sh, self.first, self.rows), 0:128], pr.at[self.sem + 2])
            to_peer(self.sh, self.first, self.rows)

    keep_other = pltpu.make_async_copy(other_p, params.at[some(other, 0, HALF), col(0)], local.at[0])
    keep_other.start()

    @pl.when(c == 0)
    def _():
        for k in range(1, 4):
            piece_y(k).start()
        for k in range(1, 4):
            piece_x(1, k, 128, 128, 13).start()

    @pl.when(c == 1)
    def _():
        for k in range(1, 4):
            piece_x(1, k, 0, 256, 3).start()

    for n in range(4):
        own_block(c, y, n)

    @pl.when(c == 0)
    def _():
        low = [RingY(other, other_p.at[128:256, :], 128, 128, 16)]
        low += [RingY(near(1, -k), None, 128, 128, 16 + 3 * k) for k in (1, 2, 3)]
        came_all(gq.at[0, 0:3], gr.at[2])
        group_c.start()
        other_blocks()
        launch_x(0)
        low[0].launch()
        for copy in keep(c, 1):
            copy.start()
        for k in range(1, 4):
            piece_x(1, k, 128, 128, 13).wait_recv()
            low[k].launch()
        relay_x(0)
        came_all(params.at[some(other, 0, 128), 0:384], pr.at[12])
        keep_other.wait()
        launch_x(1)
        to_peer(other, 0, 128)
        for k in range(4):
            low[k].relay()
        finish_x(0)
        rest()
        relay_x(1)
        for k in range(4):
            low[k].finish()
        finish_x(1)

    @pl.when(c == 1)
    def _():
        rings = [RingY(other, other_p, 0, 256, 6)]
        rings += [RingY(near(e, -k), None, 0, 256, 6 + 3 * (k + 3 * e)) for e in (0, 1) for k in (1, 2, 3)]
        for k in range(1, 4):
            piece_x(0, k, 0, 256, 0).start()
        rings[0].launch()
        for k in range(1, 4):
            group_y(k).start()
        for k in range(1, 4):
            piece_x(1, k, 0, 256, 3).wait_recv()
            rings[3 + k].launch()
        for k in range(1, 4):
            piece_x(0, k, 0, 256, 0).wait_recv()
            rings[k].launch()
        rings[0].relay()
        came_all(gq.at[0, 0:3], gr.at[2])
        group_c.start()
        other_blocks()
        for copy in keep(c, 1):
            copy.start()
        keep_other.wait()
        for n in (4, 5, 6, 1, 2, 3):
            rings[n].relay()
        rest()
        for n in (0, 4, 5, 6, 1, 2, 3):
            rings[n].finish()

    all_sent(11, gq.at[0])
    came_all(params.at[0:7 * HALF, :], kr.at[0])
    all_sent(12, params.at[0:27 * 64, :])
    all_sent(13, params.at[0:7 * HALF, :])
    for copy in keep(c, 1) + keep(1 - c, 6):
        copy.wait()
    for wait in left:
        wait()


def store(*refs):
    copies = [pltpu.make_async_copy(refs[n], refs[5 + n], refs[10].at[n]) for n in range(5)]
    for copy in copies[::-1]:
        copy.start()
    for copy in copies:
        copy.wait()


def shards(activations, out_grad, master, moment_one, moment_two, alive, step_count):
    hbm = pl.BlockSpec(memory_space=pl.ANY)
    dma = pltpu.SemaphoreType.DMA
    vm = pltpu.VMEM
    results = [((SH, KVW), F32)] * 4 + [((DW, KVW), BF16)]
    held = pl.pallas_call(
        kernel,
        out_shape=[vm(*r) for r in results],
        in_specs=[hbm] * 5 + [pl.BlockSpec(memory_space=pltpu.SMEM)] * 2,
        out_specs=[hbm] * 5,
        scratch_shapes=[
            vm((SH, KVW), F32), vm((SH, KVW), F32), vm((SH, KVW), F32), vm((SH, KVW), F32),
            vm((SH, KVW), BF16), vm((HALF, 128), BF16),
            vm((TOK, DW), BF16), vm((TOK, KVW), BF16),
            vm((SH, KVW), F32), vm((SH, KVW), F32), vm((SH, KVW), F32), vm((3, HALF, 128), F32),
            vm((8, SH, KVW), F32), vm((8, QR, KVW), I16), vm((8, QR, KVW), I16), vm((8, HALF, KVW), F32),
            vm((8, QR, KVW), I16), vm((8, QR, KVW), I16), vm((24, QR, 128), I16),
            vm((2, QR, KVW), I16), vm((2, 3, QR, 128), I16), vm((2, 3, QR, 128), I16),
            vm((HALF, KVW), F32), vm((2, HALF, 128), F32),
            vm((7, 80, 128), I16), vm((7, 80, 128), I16),
            vm((64, 128), F32), vm((2, 4, 4, 80, 128), I16), vm((4, 80, 128), I16),
            vm((8, 8, 128), F32), vm((16, 8, 128), F32), vm((2, 8, 128), F32),
            dma((12,)), dma((14,)), dma((8,)), dma((8,)), dma((2,)), dma((1,)), dma((1,)), dma((3,)), dma((4,)),
            dma((28,)), dma((1,)), dma((11,)),
        ],
        compiler_params=pltpu.CompilerParams(
            collective_id=0, has_side_effects=True, vmem_limit_bytes=50 * 2**20),
        name="reduce_update_gather",
    )(activations, out_grad, master, moment_one, moment_two, alive, step_count)
    return tuple(pl.pallas_call(
        store,
        out_shape=[jax.ShapeDtypeStruct(*r) for r in results],
        in_specs=[hbm] * 5,
        out_specs=[hbm] * 5,
        scratch_shapes=[dma((5,))],
        compiler_params=pltpu.CompilerParams(vmem_limit_bytes=2**20),
        name="store_results",
    )(*(pltpu.with_memory_space_constraint(v, vm) for v in held)))


def solution(mesh):
    return jax.shard_map(
        shards,
        mesh=mesh,
        in_specs=(
            P(("replica", "shard"), None),
            P(("replica", "shard"), None),
            P("shard", None),
            P("shard", None),
            P("shard", None),
            P(),
            P(),
        ),
        out_specs=(P("shard", None), P("shard", None), P("shard", None), P("shard", None), P()),
        check_vma=False,
    )
```

```python
import functools

import jax
import jax.numpy as jnp
from jax import lax
from jax.experimental import pallas as pl
from jax.experimental.pallas import tpu as pltpu
from jax.sharding import PartitionSpec as P

DW = 4096
KVW = 512
TOK = 1024
SH = 512
HALF = 256
QR = HALF + 16
LEVELS = 32000.0
F32 = jnp.float32
BF16 = jnp.bfloat16
I16 = jnp.int16
MESH = pl.DeviceIdType.MESH


def place():
    r = lax.axis_index("replica")
    s = lax.axis_index("shard")
    return s // 2, r // 8, (s % 2) * 4 + (r // 2) % 4, r % 2


def dev(x, y, z, c):
    return ((y * 4 + z % 4) * 2 + c, x * 2 + z // 4)


def remote(src, dst, ssem, rsem, who):
    return pltpu.make_async_remote_copy(
        src_ref=src, dst_ref=dst, send_sem=ssem, recv_sem=rsem, device_id=who, device_id_type=MESH
    )


def turn(t):
    k = 3 - t % 4
    return k + (k // 2) * (5 - 2 * k)


def span(start, size):
    return pl.ds(pl.multiple_of(start, size), size)


def step_of(code):
    return jnp.exp2(code * 0.125)


def fold_max(acc, block):
    rows, cols = block.shape
    return jnp.maximum(acc, jnp.max(jnp.abs(block).reshape(rows // 8, 8, cols), axis=0))


def code_of(largest):
    top = jnp.max(largest, axis=0, keepdims=True)
    code = jnp.clip(jnp.ceil(8.0 * jnp.log2(jnp.maximum(top, 1e-37) * (1.0 / LEVELS))), -960.0, 960.0)
    return code, step_of(-code)


def quantized(block, inverse):
    return jnp.round(block * inverse).astype(jnp.int32).astype(I16)


def code_rows(code):
    return jnp.broadcast_to(code.astype(jnp.int32), (16, code.shape[1])).astype(I16)


def encode(read, q, rows, cols, chunk, largest):
    code, inverse = code_of(largest)

    @pl.loop(0, rows // chunk, unroll=True)
    def _(i):
        at = pl.multiple_of(i * chunk, chunk)
        q[pl.ds(at, chunk), :] = quantized(read(at), inverse)

    q[pl.ds(rows, 16), :] = code_rows(code)


def step_in(q, rows):
    return step_of(q[pl.ds(rows, 16), :].astype(jnp.int32).astype(F32)[0:1, :])


def decoded(q, at, chunk, step):
    return q[pl.ds(at, chunk), :].astype(jnp.int32).astype(F32) * step


def kernel(act, grad, master, m1, m2, alive, steps, clipped_h, master_h, m1_h, m2_h, params,
           clipped_o, master_o, m1_o, m2_o, near_p, other_p, a, b, w0, w1, w2, ow, g, pq, got, own, q1s, q1rx, q1ry, q2x, q2y, q2r, full, part, q3s, q3r, block, gq, oq,
           nz, nxy, nc, asem, sent, cr, s1r, s2r, s3r, orr, nr, gr, pr, kr, local):
    x, y, z, c = place()
    zh, zl = z // 4, z % 4
    peer = dev(x, y, z, 1 - c)
    shard = x * 2 + zh
    other = x * 2 + 1 - zh
    left = []

    def at_x(k):
        return dev((x + k) % 4, y, z, c)

    def at_y(k):
        return dev(x, (y + k) % 4, z, c)

    def at_z(k):
        return dev(x, y, (z + k) % 8, c)

    def at_zl(k, h):
        return dev(x, y, (zh if h else 1 - zh) * 4 + (zl + k) % 4, c)

    xy = [(i, j) for i in range(4) for j in range(4) if (i, j) != (0, 0)]

    def at_xy(k):
        return dev((x + xy[k][0]) % 4, (y + xy[k][1]) % 4, z, c)

    def a_copy(t):
        cols = span((((x + turn(t)) % 4) * 2 + jnp.where(t < 4, 1 - zh, zh)) * SH, SH)
        return pltpu.make_async_copy(act.at[:, cols], a.at[:, cols], asem.at[t])

    b_copy = pltpu.make_async_copy(grad, b, asem.at[8])
    b_copy.start()
    for t in range(2):
        a_copy(t).start()
    state = [pltpu.make_async_copy(src, dst, asem.at[9 + n]) for n, (src, dst) in
             enumerate(((master, w0), (m1, w1), (m2, w2)))]
    weight = alive[lax.axis_index("replica")].astype(F32)

    barrier = pltpu.get_barrier_semaphore()
    pl.semaphore_signal(barrier, inc=1, device_id=peer, device_id_type=MESH)
    for k in range(15):
        pl.semaphore_signal(barrier, inc=1, device_id=at_xy(k), device_id_type=MESH)
    for k in range(1, 8):
        pl.semaphore_signal(barrier, inc=1, device_id=at_z(k), device_id_type=MESH)

    b_copy.wait()
    def core_copy(t):
        return remote(pq.at[t], got.at[t], sent.at[0], cr.at[t], peer)

    def wait_for(t):
        a_copy(t).wait()

    def product(t):
        cols = span((((x + turn(t)) % 4) * 2 + jnp.where(t < 4, 1 - zh, zh)) * SH, SH)
        g[t] = lax.dot_general(a[:, cols], b[...], (((0,), (0,)), ((), ())), preferred_element_type=F32)

    def first_x(t):
        return remote(q1s.at[t], q1rx.at[t], sent.at[1], s1r.at[t], at_x(turn(t)))

    def first_y(t, j):
        return remote(q1s.at[t, :, span(((y + j + 1) % 4) * 128, 128)], q1ry.at[t * 3 + j], sent.at[1],
                      s1r.at[t], at_y(j + 1))

    def for_peer(t):
        largest = jnp.zeros((8, KVW), F32)
        for n in range(8):
            largest = fold_max(largest, g[t, span((1 - c) * HALF + n * 32, 32), :])
        code, inverse = code_of(largest * weight)
        inverse = inverse * weight
        for n in range(8):
            pq[t, n * 32:(n + 1) * 32, :] = quantized(g[t, span((1 - c) * HALF + n * 32, 32), :], inverse)
        pq[t, HALF:QR, :] = code_rows(code)

    def summed(t):
        largest = jnp.zeros((8, KVW), F32)
        step = step_in(got.at[t], HALF)
        for n in range(8):
            rows = span(c * HALF + n * 32, 32)
            total = g[t, rows, :] * weight + decoded(got.at[t], n * 32, 32, step)
            own[t, n * 32:(n + 1) * 32, :] = total
            largest = fold_max(largest, total)
        return largest

    def coded(t, largest):
        code, inverse = code_of(largest)
        for n in range(8):
            q1s[t, n * 32:(n + 1) * 32, :] = quantized(own[t, n * 32:(n + 1) * 32, :], inverse)
        q1s[t, HALF:QR, :] = code_rows(code)

    def send(t):
        @pl.when(jnp.logical_and(c == 0, t % 4 < 3))
        def _():
            first_x(t).start()

        @pl.when(c == 1)
        def _():
            for j in range(3):
                first_y(t, j).start()

    wait_for(0)
    for t in range(2, 8):
        a_copy(t).start()
    product(0)
    for_peer(0)
    pl.semaphore_wait(barrier, 23)
    core_copy(0).start()
    piece = (span(c * HALF, HALF), span(y * 128, 128))
    lend = [remote(src.at[piece[0], piece[1]], ow.at[n], sent.at[2], orr.at[0], at_z(4)) for n, src in
            enumerate((master, m1, m2))]
    for copy in lend:
        copy.start()

    @pl.loop(1, 8)
    def _(t):
        wait_for(t)
        product(t)
        for_peer(t)
        core_copy(t).start()
        core_copy(t - 1).wait_recv()
        coded(t - 1, summed(t - 1))
        send(t - 1)

    core_copy(7).wait_recv()
    coded(7, summed(7))
    send(7)
    for copy in state:
        copy.start()
    def all_sent(sem, ref):
        left.append(remote(ref, ref, sent.at[sem], sent.at[sem], peer).wait_send)

    def came_all(ref, sem):
        remote(ref, ref, sent.at[0], sem, peer).wait_recv()

    all_sent(0, pq)
    all_sent(1, q1s.at[0:6])
    all_sent(2, ow)

    def second_y(h, j):
        return remote(q2x.at[h, :, span(((y + j + 1) % 4) * 128, 128)], q2r.at[h, j], sent.at[3],
                      s2r.at[h], at_y(j + 1))

    def second_x(h, i):
        return remote(q2y.at[h, i], q2r.at[h, i], sent.at[3], s2r.at[h], at_x(turn(i)))

    def first_sums(h):
        @pl.when(c == 0)
        def _():
            for i in range(3):
                first_x(h * 4 + i).wait_recv()
            step = [step_in(q1rx.at[h * 4 + i], HALF) for i in range(3)]

            def add(n, acc):
                at = pl.multiple_of(n * 32, 32)
                total = own[h * 4 + 3, pl.ds(at, 32), :]
                for i in range(3):
                    total += decoded(q1rx.at[h * 4 + i], at, 32, step[i])
                full[pl.ds(at, 32), :] = total
                return fold_max(acc, total)

            largest = lax.fori_loop(0, HALF // 32, add, jnp.zeros((8, KVW), F32))
            encode(lambda at: full[pl.ds(at, 32), :], q2x.at[h], HALF, KVW, 32, largest)
            for j in range(3):
                second_y(h, j).start()
            part[h] = full[:, span(y * 128, 128)]

        @pl.when(c == 1)
        def _():
            @pl.loop(0, 4)
            def _(i):
                t = h * 4 + i
                came_all(q1ry.at[pl.ds(t * 3, 3)], s1r.at[t])
                step = [step_in(q1ry.at[t * 3 + j], HALF) for j in range(3)]

                def add(n, acc):
                    at = pl.multiple_of(n * 128, 128)
                    total = own[t, pl.ds(at, 128), span(y * 128, 128)]
                    for j in range(3):
                        total += decoded(q1ry.at[t * 3 + j], at, 128, step[j])
                    part[h, pl.ds(at, 128), :] = total
                    return fold_max(acc, total)

                largest = lax.fori_loop(0, 2, add, jnp.zeros((8, 128), F32))

                @pl.when(i < 3)
                def _():
                    encode(lambda at: part[h, pl.ds(at, 128), :], q2y.at[h, i], HALF, 128, 128, largest)
                    second_x(h, i).start()

    def third(h, k):
        n = h * 3 + k
        return remote(q3s.at[n], q3r.at[n], sent.at[4], s3r.at[0], at_zl(k, h))

    def second_sums(h):
        came_all(q2r.at[h], s2r.at[h])
        step = [step_in(q2r.at[h, j], HALF) for j in range(3)]
        largest = jnp.zeros((8, 128), F32)
        for n in range(4):
            at = n * 64
            total = part[h, at:at + 64, :]
            for j in range(3):
                total += decoded(q2r.at[h, j], at, 64, step[j])
            part[h, at:at + 64, :] = total
            largest = fold_max(largest, total)
        code, inverse = code_of(largest)
        for k in range(h, 4):
            q3s[h * 3 + k, 0:64, :] = quantized(part[h, span(((zl + k) % 4) * 64, 64), :], inverse)
            q3s[h * 3 + k, 64:80, :] = code_rows(code)
        for k in range(h, 4):
            third(h, k).start()

    all_sent(3, q2r)
    all_sent(4, q3s)
    first_sums(0)
    second_sums(0)
    first_sums(1)
    second_sums(1)
    total = part[1, span(zl * 64, 64), :]
    came_all(q3r, s3r.at[0])
    for n in range(7):
        total += decoded(q3r.at[n], 0, 64, step_in(q3r.at[n], 64))

    mine = gq.at[c, y, zl]
    def tell_z(k):
        return remote(nz.at[z], nz.at[z], sent.at[5], nr.at[0], at_z(k))

    def tell_xy(k):
        slot = nxy.at[x * 4 + y]
        return remote(slot, slot, sent.at[6], nr.at[1], at_xy(k))

    tell_c = remote(nc.at[c], nc.at[c], sent.at[7], nr.at[2], peer)

    def group_z(k):
        return remote(mine, mine, sent.at[8], gr.at[0], at_zl(k, 1))

    def cross_z(k):
        return remote(mine, oq.at[zl], sent.at[9], gr.at[1], at_zl(k, 0))

    def group_y(k):
        return remote(gq.at[c, y], gq.at[c, y], sent.at[10], gr.at[2], at_y(k))

    group_c = remote(gq.at[c], gq.at[c], sent.at[11], gr.at[3], peer)

    nz[z] = jnp.sum((total * total).reshape(8, 8, 128), axis=0)
    for k in range(1, 8):
        tell_z(k).start()
    encode(lambda at: total, mine, 64, 128, 64, fold_max(jnp.zeros((8, 128), F32), total))
    for k in range(1, 4):
        group_z(k).start()
    came_all(nz.at[0:7], nr.at[0])
    nxy[x * 4 + y] = jnp.sum(nz[...], axis=0)
    for k in range(15):
        tell_xy(k).start()
    for k in range(4):
        cross_z(k).start()
    came_all(gq.at[0, 0, 0:3], gr.at[0])

    @pl.when(c == 0)
    def _():
        for k in range(1, 4):
            group_y(k).start()

    came_all(nxy.at[0:15], nr.at[1])
    nc[c] = jnp.sum(nxy[...], axis=0)
    tell_c.start()
    for copy in state:
        copy.wait()
    came_all(ow, orr.at[0])
    came_all(oq, gr.at[1])
    tell_c.wait_recv()
    square = jnp.sum(nc[0] + nc[1], keepdims=True)
    factor = jnp.minimum(1.0, jnp.sqrt(F32(DW * KVW)) / jnp.sqrt(square + 1e-06))

    all_sent(5, nz.at[0:7])
    all_sent(6, nxy.at[0:15])
    all_sent(7, nc.at[0])
    all_sent(8, gq.at[0, 0, 0:3])
    all_sent(9, oq)
    all_sent(10, gq.at[0, 0:3])

    done = jnp.full((1, 128), steps[0].astype(F32))
    correct1 = 1.0 / (1.0 - jnp.exp(done * jnp.log(F32(0.9))))
    correct2 = 1.0 / (1.0 - jnp.exp(done * jnp.log(F32(0.95))))

    def adam(q, old, one, two):
        clipped = decoded(q, 0, 64, step_in(q, 64)) * factor
        one = 0.9 * one + 0.1 * clipped
        two = 0.95 * two + 0.05 * clipped * clipped
        new = old - 0.01 * ((one * correct1) / (jnp.sqrt(two * correct2) + 1e-08) + 0.1 * old)
        return clipped, new, one, two

    def col(k):
        return span(((y + k + 4) % 4) * 128, 128)

    for n in range(4):
        rows = pl.ds(n * 64, 64)
        new = adam(oq.at[n], ow[0, rows, :], ow[1, rows, :], ow[2, rows, :])[1]
        other_p[n * 64:(n + 1) * 64, :] = new.astype(BF16)

    rows_c = span(c * HALF, HALF)

    def own_block(cc, yy, zz):
        rows = span(cc * HALF + zz * 64, 64)
        cols = span(yy * 128, 128)
        clipped, new, one, two = adam(gq.at[cc, yy, zz], w0[rows, cols], w1[rows, cols], w2[rows, cols])
        clipped_o[rows, cols] = clipped
        master_o[rows, cols] = new
        m1_o[rows, cols] = one
        m2_o[rows, cols] = two
        near_p[rows, cols] = new.astype(BF16)

    def other_blocks():
        @pl.loop(0, 12, unroll=4)
        def _(n):
            own_block(c, (y + 1 + n // 4) % 4, n % 4)

    outs = [(clipped_o, clipped_h), (master_o, master_h), (m1_o, m1_h), (m2_o, m2_h)]

    def keep(cc, n):
        rows = span(cc * HALF, HALF)
        copies = [pltpu.make_async_copy(src.at[rows, :], dst.at[rows, :], local.at[n + i]) for i, (src, dst) in enumerate(outs)]
        there = params.at[span(shard * SH + cc * HALF, HALF), :]
        return copies + [pltpu.make_async_copy(near_p.at[rows, :], there, local.at[n + 4])]

    def rest():
        group_c.wait_recv()

        @pl.loop(0, 16, unroll=4)
        def _(n):
            own_block(1 - c, n // 4, n % 4)

        for copy in keep(1 - c, 6):
            copy.start()

    def near(e, k):
        return ((x + k + 4) % 4) * 2 + (1 - zh if e else zh)

    def some(sh, first, rows):
        return pl.ds(pl.multiple_of(sh * SH + c * HALF + first, 64), rows)

    def to_peer(sh, first, rows):
        ref = params.at[some(sh, first, rows), :]
        remote(ref, ref, sent.at[13], kr.at[0], peer).start()

    def gather(src, dst, sem, who):
        return remote(src, dst, sent.at[12], pr.at[sem], who)

    def piece_x(e, k, first, rows, sem):
        src = other_p.at[first:first + rows, :] if e else near_p.at[some(0, first, rows), col(0)]
        return gather(src, params.at[some(near(e, 0), first, rows), col(0)], sem + k - 1, at_x(k))

    def piece_y(k):
        return gather(other_p.at[0:128, :], params.at[some(other, 0, 128), col(0)], 12, at_y(k))

    def ring_x(e, n):
        owner, lower, way = ((0, 0, 1), (0, 1, 1), (0, 1, 3), (0, 0, 3), (-1, 0, 1), (1, 1, 3))[n]
        rows = 64 if e else 128
        ref = params.at[some(near(e, owner), lower * rows, rows), :]
        src = near_p.at[some(0, lower * rows, rows), :] if e == 0 and n < 4 else ref
        return gather(src, ref, e * 6 + n, at_x(way))

    def launch_x(e):
        for n in (0, 2, 1, 3):
            ring_x(e, n).start()

    def relay_x(e):
        rows = 64 if e else 128
        ring_x(e, 0).wait_recv()
        ring_x(e, 4).start()
        ring_x(e, 2).wait_recv()
        ring_x(e, 5).start()
        to_peer(near(e, -1), 0, rows)
        to_peer(near(e, 1), rows, rows)

    def finish_x(e):
        rows = 64 if e else 128
        for n, owner, lower in ((1, -1, 1), (3, 1, 0), (4, 2, 0), (5, 2, 1)):
            ring_x(e, n).wait_recv()
            to_peer(near(e, owner), lower * rows, rows)

    class RingY:
        def __init__(self, sh, src, first, rows, sem):
            self.sh, self.src, self.first, self.rows, self.sem = sh, src, first, rows, sem

        def copy(self, m):
            owner, lower, part, way = ((0, 0, 1, 1), (0, 0, 1, 3), (-1, 0, 2, 1), (1, 1, 2, 3))[m]
            size = self.rows // part
            ref = params.at[some(self.sh, self.first + lower * size, size), col(owner)]
            src = self.src if self.src is not None and m < 2 else ref
            return gather(src, ref, self.sem + min(m, 2), at_y(way))

        def launch(self):
            self.copy(0).start()
            self.copy(1).start()

        def relay(self):
            self.copy(0).wait_recv()
            self.copy(2).start()
            self.copy(1).wait_recv()
            self.copy(3).start()

        def finish(self):
            came_all(params.at[some(self.sh, self.first, self.rows), 0:128], pr.at[self.sem + 2])
            to_peer(self.sh, self.first, self.rows)

    keep_other = pltpu.make_async_copy(other_p, params.at[some(other, 0, HALF), col(0)], local.at[0])
    keep_other.start()

    @pl.when(c == 0)
    def _():
        for k in range(1, 4):
            piece_y(k).start()
        for k in range(1, 4):
            piece_x(1, k, 128, 128, 13).start()

    @pl.when(c == 1)
    def _():
        for k in range(1, 4):
            piece_x(1, k, 0, 256, 3).start()

    for n in range(4):
        own_block(c, y, n)

    @pl.when(c == 0)
    def _():
        low = [RingY(other, other_p.at[128:256, :], 128, 128, 16)]
        low += [RingY(near(1, -k), None, 128, 128, 16 + 3 * k) for k in (1, 2, 3)]
        came_all(gq.at[0, 0:3], gr.at[2])
        group_c.start()
        other_blocks()
        launch_x(0)
        low[0].launch()
        for copy in keep(c, 1):
            copy.start()
        for k in range(1, 4):
            piece_x(1, k, 128, 128, 13).wait_recv()
            low[k].launch()
        relay_x(0)
        came_all(params.at[some(other, 0, 128), 0:384], pr.at[12])
        keep_other.wait()
        launch_x(1)
        to_peer(other, 0, 128)
        for k in range(4):
            low[k].relay()
        finish_x(0)
        rest()
        relay_x(1)
        for k in range(4):
            low[k].finish()
        finish_x(1)

    @pl.when(c == 1)
    def _():
        rings = [RingY(other, other_p, 0, 256, 6)]
        rings += [RingY(near(e, -k), None, 0, 256, 6 + 3 * (k + 3 * e)) for e in (0, 1) for k in (1, 2, 3)]
        for k in range(1, 4):
            piece_x(0, k, 0, 256, 0).start()
        rings[0].launch()
        for k in range(1, 4):
            group_y(k).start()
        for k in range(1, 4):
            piece_x(1, k, 0, 256, 3).wait_recv()
            rings[3 + k].launch()
        for k in range(1, 4):
            piece_x(0, k, 0, 256, 0).wait_recv()
            rings[k].launch()
        rings[0].relay()
        came_all(gq.at[0, 0:3], gr.at[2])
        group_c.start()
        other_blocks()
        for copy in keep(c, 1):
            copy.start()
        keep_other.wait()
        for n in (4, 5, 6, 1, 2, 3):
            rings[n].relay()
        rest()
        for n in (0, 4, 5, 6, 1, 2, 3):
            rings[n].finish()

    all_sent(11, gq.at[0])
    came_all(params.at[0:7 * HALF, :], kr.at[0])
    all_sent(12, params.at[0:27 * 64, :])
    all_sent(13, params.at[0:7 * HALF, :])
    for copy in keep(c, 1) + keep(1 - c, 6):
        copy.wait()
    for wait in left:
        wait()


def store(*refs):
    copies = [pltpu.make_async_copy(refs[n], refs[5 + n], refs[10].at[n]) for n in range(5)]
    for copy in copies[::-1]:
        copy.start()
    for copy in copies:
        copy.wait()


def shards(activations, out_grad, master, moment_one, moment_two, alive, step_count):
    hbm = pl.BlockSpec(memory_space=pl.ANY)
    dma = pltpu.SemaphoreType.DMA
    vm = pltpu.VMEM
    results = [((SH, KVW), F32)] * 4 + [((DW, KVW), BF16)]
    held = pl.pallas_call(
        kernel,
        out_shape=[vm(*r) for r in results],
        in_specs=[hbm] * 5 + [pl.BlockSpec(memory_space=pltpu.SMEM)] * 2,
        out_specs=[hbm] * 5,
        scratch_shapes=[
            vm((SH, KVW), F32), vm((SH, KVW), F32), vm((SH, KVW), F32), vm((SH, KVW), F32),
            vm((SH, KVW), BF16), vm((HALF, 128), BF16),
            vm((TOK, DW), BF16), vm((TOK, KVW), BF16),
            vm((SH, KVW), F32), vm((SH, KVW), F32), vm((SH, KVW), F32), vm((3, HALF, 128), F32),
            vm((8, SH, KVW), F32), vm((8, QR, KVW), I16), vm((8, QR, KVW), I16), vm((8, HALF, KVW), F32),
            vm((8, QR, KVW), I16), vm((8, QR, KVW), I16), vm((24, QR, 128), I16),
            vm((2, QR, KVW), I16), vm((2, 3, QR, 128), I16), vm((2, 3, QR, 128), I16),
            vm((HALF, KVW), F32), vm((2, HALF, 128), F32),
            vm((7, 80, 128), I16), vm((7, 80, 128), I16),
            vm((64, 128), F32), vm((2, 4, 4, 80, 128), I16), vm((4, 80, 128), I16),
            vm((8, 8, 128), F32), vm((16, 8, 128), F32), vm((2, 8, 128), F32),
            dma((12,)), dma((14,)), dma((8,)), dma((8,)), dma((2,)), dma((1,)), dma((1,)), dma((3,)), dma((4,)),
            dma((28,)), dma((1,)), dma((11,)),
        ],
        compiler_params=pltpu.CompilerParams(
            collective_id=0, has_side_effects=True, vmem_limit_bytes=50 * 2**20),
        name="reduce_update_gather",
    )(activations, out_grad, master, moment_one, moment_two, alive, step_count)
    return tuple(pl.pallas_call(
        store,
        out_shape=[jax.ShapeDtypeStruct(*r) for r in results],
        in_specs=[hbm] * 5,
        out_specs=[hbm] * 5,
        scratch_shapes=[dma((5,))],
        compiler_params=pltpu.CompilerParams(vmem_limit_bytes=2**20),
        name="store_results",
    )(*(pltpu.with_memory_space_constraint(v, vm) for v in held)))


def solution(mesh):
    return jax.shard_map(
        shards,
        mesh=mesh,
        in_specs=(
            P(("replica", "shard"), None),
            P(("replica", "shard"), None),
            P("shard", None),
            P("shard", None),
            P("shard", None),
            P(),
            P(),
        ),
        out_specs=(P("shard", None), P("shard", None), P("shard", None), P("shard", None), P()),
        check_vma=False,
    )
```

```python
import functools

import jax
import jax.numpy as jnp
from jax import lax
from jax.experimental import pallas as pl
from jax.experimental.pallas import tpu as pltpu
from jax.sharding import PartitionSpec as P

DW = 4096
KVW = 512
TOK = 1024
SH = 512
HALF = 256
QR = HALF + 16
LEVELS = 32000.0
F32 = jnp.float32
BF16 = jnp.bfloat16
I16 = jnp.int16
MESH = pl.DeviceIdType.MESH


def place():
    r = lax.axis_index("replica")
    s = lax.axis_index("shard")
    return s // 2, r // 8, (s % 2) * 4 + (r // 2) % 4, r % 2


def dev(x, y, z, c):
    return ((y * 4 + z % 4) * 2 + c, x * 2 + z // 4)


def remote(src, dst, ssem, rsem, who):
    return pltpu.make_async_remote_copy(
        src_ref=src, dst_ref=dst, send_sem=ssem, recv_sem=rsem, device_id=who, device_id_type=MESH
    )


def turn(t):
    k = 3 - t % 4
    return k + (k // 2) * (5 - 2 * k)


def span(start, size):
    return pl.ds(pl.multiple_of(start, size), size)


def step_of(code):
    return jnp.exp2(code * 0.125)


def fold_max(acc, block):
    rows, cols = block.shape
    return jnp.maximum(acc, jnp.max(jnp.abs(block).reshape(rows // 8, 8, cols), axis=0))


def code_of(largest):
    top = jnp.max(largest, axis=0, keepdims=True)
    code = jnp.clip(jnp.ceil(8.0 * jnp.log2(jnp.maximum(top, 1e-37) * (1.0 / LEVELS))), -960.0, 960.0)
    return code, step_of(-code)


def quantized(block, inverse):
    return jnp.round(block * inverse).astype(jnp.int32).astype(I16)


def code_rows(code):
    return jnp.broadcast_to(code.astype(jnp.int32), (16, code.shape[1])).astype(I16)


def encode(read, q, rows, cols, chunk, largest):
    code, inverse = code_of(largest)

    @pl.loop(0, rows // chunk, unroll=True)
    def _(i):
        at = pl.multiple_of(i * chunk, chunk)
        q[pl.ds(at, chunk), :] = quantized(read(at), inverse)

    q[pl.ds(rows, 16), :] = code_rows(code)


def step_in(q, rows):
    return step_of(q[pl.ds(rows, 16), :].astype(jnp.int32).astype(F32)[0:1, :])


def decoded(q, at, chunk, step):
    return q[pl.ds(at, chunk), :].astype(jnp.int32).astype(F32) * step


def kernel(act, grad, master, m1, m2, alive, steps, clipped_h, master_h, m1_h, m2_h, params,
           clipped_o, master_o, m1_o, m2_o, near_p, other_p, a, b, w0, w1, w2, ow, g, pq, got, own, q1s, q1rx, q1ry, q2x, q2y, q2r, full, part, q3s, q3r, block, gq, oq,
           nz, nxy, nc, asem, sent, cr, s1r, s2r, s3r, orr, nr, gr, pr, kr, local):
    x, y, z, c = place()
    zh, zl = z // 4, z % 4
    peer = dev(x, y, z, 1 - c)
    shard = x * 2 + zh
    other = x * 2 + 1 - zh
    left = []

    def at_x(k):
        return dev((x + k) % 4, y, z, c)

    def at_y(k):
        return dev(x, (y + k) % 4, z, c)

    def at_z(k):
        return dev(x, y, (z + k) % 8, c)

    def at_zl(k, h):
        return dev(x, y, (zh if h else 1 - zh) * 4 + (zl + k) % 4, c)

    xy = [(i, j) for i in range(4) for j in range(4) if (i, j) != (0, 0)]

    def at_xy(k):
        return dev((x + xy[k][0]) % 4, (y + xy[k][1]) % 4, z, c)

    def a_copy(t):
        cols = span((((x + turn(t)) % 4) * 2 + jnp.where(t < 4, 1 - zh, zh)) * SH, SH)
        return pltpu.make_async_copy(act.at[:, cols], a.at[:, cols], asem.at[t])

    b_copy = pltpu.make_async_copy(grad, b, asem.at[8])
    b_copy.start()
    for t in range(2):
        a_copy(t).start()
    state = [pltpu.make_async_copy(src, dst, asem.at[9 + n]) for n, (src, dst) in
             enumerate(((master, w0), (m1, w1), (m2, w2)))]
    weight = alive[lax.axis_index("replica")].astype(F32)

    barrier = pltpu.get_barrier_semaphore()
    pl.semaphore_signal(barrier, inc=1, device_id=peer, device_id_type=MESH)
    for k in range(15):
        pl.semaphore_signal(barrier, inc=1, device_id=at_xy(k), device_id_type=MESH)
    for k in range(1, 8):
        pl.semaphore_signal(barrier, inc=1, device_id=at_z(k), device_id_type=MESH)

    b_copy.wait()
    def core_copy(t):
        return remote(pq.at[t], got.at[t], sent.at[0], cr.at[t], peer)

    def wait_for(t):
        a_copy(t).wait()

    def product(t):
        cols = span((((x + turn(t)) % 4) * 2 + jnp.where(t < 4, 1 - zh, zh)) * SH, SH)
        g[t] = lax.dot_general(a[:, cols], b[...], (((0,), (0,)), ((), ())), preferred_element_type=F32)

    def first_x(t):
        return remote(q1s.at[t], q1rx.at[t], sent.at[1], s1r.at[t], at_x(turn(t)))

    def first_y(t, j):
        return remote(q1s.at[t, :, span(((y + j + 1) % 4) * 128, 128)], q1ry.at[t * 3 + j], sent.at[1],
                      s1r.at[t], at_y(j + 1))

    def for_peer(t):
        largest = jnp.zeros((8, KVW), F32)
        for n in range(8):
            largest = fold_max(largest, g[t, span((1 - c) * HALF + n * 32, 32), :])
        code, inverse = code_of(largest * weight)
        inverse = inverse * weight
        for n in range(8):
            pq[t, n * 32:(n + 1) * 32, :] = quantized(g[t, span((1 - c) * HALF + n * 32, 32), :], inverse)
        pq[t, HALF:QR, :] = code_rows(code)

    def summed(t):
        largest = jnp.zeros((8, KVW), F32)
        step = step_in(got.at[t], HALF)
        for n in range(8):
            rows = span(c * HALF + n * 32, 32)
            total = g[t, rows, :] * weight + decoded(got.at[t], n * 32, 32, step)
            own[t, n * 32:(n + 1) * 32, :] = total
            largest = fold_max(largest, total)
        return largest

    def coded(t, largest):
        code, inverse = code_of(largest)
        for n in range(8):
            q1s[t, n * 32:(n + 1) * 32, :] = quantized(own[t, n * 32:(n + 1) * 32, :], inverse)
        q1s[t, HALF:QR, :] = code_rows(code)

    def send(t):
        @pl.when(jnp.logical_and(c == 0, t % 4 < 3))
        def _():
            first_x(t).start()

        @pl.when(c == 1)
        def _():
            for j in range(3):
                first_y(t, j).start()

    wait_for(0)
    for t in range(2, 8):
        a_copy(t).start()
    product(0)
    for_peer(0)
    pl.semaphore_wait(barrier, 23)
    core_copy(0).start()
    piece = (span(c * HALF, HALF), span(y * 128, 128))
    lend = [remote(src.at[piece[0], piece[1]], ow.at[n], sent.at[2], orr.at[0], at_z(4)) for n, src in
            enumerate((master, m1, m2))]
    for copy in lend:
        copy.start()

    @pl.loop(1, 8)
    def _(t):
        wait_for(t)
        product(t)
        for_peer(t)
        core_copy(t).start()
        core_copy(t - 1).wait_recv()
        coded(t - 1, summed(t - 1))
        send(t - 1)

    core_copy(7).wait_recv()
    coded(7, summed(7))
    send(7)
    for copy in state:
        copy.start()
    def all_sent(sem, ref):
        left.append(remote(ref, ref, sent.at[sem], sent.at[sem], peer).wait_send)

    def came_all(ref, sem):
        remote(ref, ref, sent.at[0], sem, peer).wait_recv()

    all_sent(0, pq)
    all_sent(1, q1s.at[0:6])
    all_sent(2, ow)

    def second_y(h, j):
        return remote(q2x.at[h, :, span(((y + j + 1) % 4) * 128, 128)], q2r.at[h, j], sent.at[3],
                      s2r.at[h], at_y(j + 1))

    def second_x(h, i):
        return remote(q2y.at[h, i], q2r.at[h, i], sent.at[3], s2r.at[h], at_x(turn(i)))

    def first_sums(h):
        @pl.when(c == 0)
        def _():
            for i in range(3):
                first_x(h * 4 + i).wait_recv()
            step = [step_in(q1rx.at[h * 4 + i], HALF) for i in range(3)]

            def add(n, acc):
                at = pl.multiple_of(n * 32, 32)
                total = own[h * 4 + 3, pl.ds(at, 32), :]
                for i in range(3):
                    total += decoded(q1rx.at[h * 4 + i], at, 32, step[i])
                full[pl.ds(at, 32), :] = total
                return fold_max(acc, total)

            largest = lax.fori_loop(0, HALF // 32, add, jnp.zeros((8, KVW), F32))
            encode(lambda at: full[pl.ds(at, 32), :], q2x.at[h], HALF, KVW, 32, largest)
            for j in range(3):
                second_y(h, j).start()
            part[h] = full[:, span(y * 128, 128)]

        @pl.when(c == 1)
        def _():
            @pl.loop(0, 4)
            def _(i):
                t = h * 4 + i
                came_all(q1ry.at[pl.ds(t * 3, 3)], s1r.at[t])
                step = [step_in(q1ry.at[t * 3 + j], HALF) for j in range(3)]

                def add(n, acc):
                    at = pl.multiple_of(n * 128, 128)
                    total = own[t, pl.ds(at, 128), span(y * 128, 128)]
                    for j in range(3):
                        total += decoded(q1ry.at[t * 3 + j], at, 128, step[j])
                    part[h, pl.ds(at, 128), :] = total
                    return fold_max(acc, total)

                largest = lax.fori_loop(0, 2, add, jnp.zeros((8, 128), F32))

                @pl.when(i < 3)
                def _():
                    encode(lambda at: part[h, pl.ds(at, 128), :], q2y.at[h, i], HALF, 128, 128, largest)
                    second_x(h, i).start()

    def third(h, k):
        n = h * 3 + k
        return remote(q3s.at[n], q3r.at[n], sent.at[4], s3r.at[0], at_zl(k, h))

    def second_sums(h):
        came_all(q2r.at[h], s2r.at[h])
        step = [step_in(q2r.at[h, j], HALF) for j in range(3)]
        largest = jnp.zeros((8, 128), F32)
        for n in range(4):
            at = n * 64
            total = part[h, at:at + 64, :]
            for j in range(3):
                total += decoded(q2r.at[h, j], at, 64, step[j])
            part[h, at:at + 64, :] = total
            largest = fold_max(largest, total)
        code, inverse = code_of(largest)
        for k in range(h, 4):
            q3s[h * 3 + k, 0:64, :] = quantized(part[h, span(((zl + k) % 4) * 64, 64), :], inverse)
            q3s[h * 3 + k, 64:80, :] = code_rows(code)
        for k in range(h, 4):
            third(h, k).start()

    all_sent(3, q2r)
    all_sent(4, q3s)
    first_sums(0)
    second_sums(0)
    first_sums(1)
    second_sums(1)
    total = part[1, span(zl * 64, 64), :]
    came_all(q3r, s3r.at[0])
    for n in range(7):
        total += decoded(q3r.at[n], 0, 64, step_in(q3r.at[n], 64))

    mine = gq.at[c, y, zl]
    def tell_z(k):
        return remote(nz.at[z], nz.at[z], sent.at[5], nr.at[0], at_z(k))

    def tell_xy(k):
        slot = nxy.at[x * 4 + y]
        return remote(slot, slot, sent.at[6], nr.at[1], at_xy(k))

    tell_c = remote(nc.at[c], nc.at[c], sent.at[7], nr.at[2], peer)

    def group_z(k):
        return remote(mine, mine, sent.at[8], gr.at[0], at_zl(k, 1))

    def cross_z(k):
        return remote(mine, oq.at[zl], sent.at[9], gr.at[1], at_zl(k, 0))

    def group_y(k):
        return remote(gq.at[c, y], gq.at[c, y], sent.at[10], gr.at[2], at_y(k))

    group_c = remote(gq.at[c], gq.at[c], sent.at[11], gr.at[3], peer)

    nxy[x * 4 + y] = jnp.sum((total * total).reshape(8, 8, 128), axis=0)
    for k in range(15):
        tell_xy(k).start()
    encode(lambda at: total, mine, 64, 128, 64, fold_max(jnp.zeros((8, 128), F32), total))
    for k in range(1, 4):
        group_z(k).start()
    for k in range(4):
        cross_z(k).start()
    came_all(nxy.at[0:15], nr.at[1])
    nz[z] = jnp.sum(nxy[...], axis=0)
    for k in range(1, 8):
        tell_z(k).start()
    came_all(gq.at[0, 0, 0:3], gr.at[0])

    for k in range(1, 4):
        group_y(k).start()
    came_all(nz.at[0:7], nr.at[0])
    nc[c] = jnp.sum(nz[...], axis=0)
    tell_c.start()
    for copy in state:
        copy.wait()
    came_all(ow, orr.at[0])
    came_all(oq, gr.at[1])
    tell_c.wait_recv()
    square = jnp.sum(nc[0] + nc[1], keepdims=True)
    factor = jnp.minimum(1.0, jnp.sqrt(F32(DW * KVW)) / jnp.sqrt(square + 1e-06))

    all_sent(5, nz.at[0:7])
    all_sent(6, nxy.at[0:15])
    all_sent(7, nc.at[0])
    all_sent(8, gq.at[0, 0, 0:3])
    all_sent(9, oq)
    all_sent(10, gq.at[0, 0:3])

    done = jnp.broadcast_to(steps[...].astype(F32), (1, 128))
    correct1 = 1.0 / (1.0 - jnp.exp(done * jnp.log(F32(0.9))))
    correct2 = 1.0 / (1.0 - jnp.exp(done * jnp.log(F32(0.95))))

    def adam(q, old, one, two):
        clipped = decoded(q, 0, 64, step_in(q, 64)) * factor
        one = 0.9 * one + 0.1 * clipped
        two = 0.95 * two + 0.05 * clipped * clipped
        new = old - 0.01 * ((one * correct1) / (jnp.sqrt(two * correct2) + 1e-08) + 0.1 * old)
        return clipped, new, one, two

    def col(k):
        return span(((y + k + 4) % 4) * 128, 128)

    for n in range(4):
        rows = pl.ds(n * 64, 64)
        new = adam(oq.at[n], ow[0, rows, :], ow[1, rows, :], ow[2, rows, :])[1]
        other_p[n * 64:(n + 1) * 64, :] = new.astype(BF16)

    rows_c = span(c * HALF, HALF)

    def own_block(cc, yy, zz):
        rows = span(cc * HALF + zz * 64, 64)
        cols = span(yy * 128, 128)
        clipped, new, one, two = adam(gq.at[cc, yy, zz], w0[rows, cols], w1[rows, cols], w2[rows, cols])
        clipped_o[rows, cols] = clipped
        master_o[rows, cols] = new
        m1_o[rows, cols] = one
        m2_o[rows, cols] = two
        near_p[rows, cols] = new.astype(BF16)

    def other_blocks():
        @pl.loop(0, 12, unroll=4)
        def _(n):
            own_block(c, (y + 1 + n // 4) % 4, n % 4)

    outs = [(clipped_o, clipped_h), (master_o, master_h), (m1_o, m1_h), (m2_o, m2_h)]

    def keep(cc, n):
        rows = span(cc * HALF, HALF)
        copies = [pltpu.make_async_copy(src.at[rows, :], dst.at[rows, :], local.at[n + i]) for i, (src, dst) in enumerate(outs)]
        there = params.at[span(shard * SH + cc * HALF, HALF), :]
        return copies + [pltpu.make_async_copy(near_p.at[rows, :], there, local.at[n + 4])]

    def rest():
        group_c.wait_recv()

        @pl.loop(0, 16, unroll=4)
        def _(n):
            own_block(1 - c, n // 4, n % 4)

        for copy in keep(1 - c, 6):
            copy.start()

    def near(e, k):
        return ((x + k + 4) % 4) * 2 + (1 - zh if e else zh)

    def some(sh, first, rows):
        return pl.ds(pl.multiple_of(sh * SH + c * HALF + first, 64), rows)

    def to_peer(sh, first, rows):
        ref = params.at[some(sh, first, rows), :]
        remote(ref, ref, sent.at[13], kr.at[0], peer).start()

    def gather(src, dst, sem, who):
        return remote(src, dst, sent.at[12], pr.at[sem], who)

    def piece_x(e, k, first, rows, sem):
        src = other_p.at[first:first + rows, :] if e else near_p.at[some(0, first, rows), col(0)]
        return gather(src, params.at[some(near(e, 0), first, rows), col(0)], sem + k - 1, at_x(k))

    def ring_x(e, n):
        owner, lower, way = ((0, 0, 1), (0, 1, 1), (0, 1, 3), (0, 0, 3), (-1, 0, 1), (1, 1, 3))[n]
        rows = 64 if e else 128
        ref = params.at[some(near(e, owner), lower * rows, rows), :]
        src = near_p.at[some(0, lower * rows, rows), :] if e == 0 and n < 4 else ref
        return gather(src, ref, e * 6 + n, at_x(way))

    def launch_x(e):
        for n in (0, 2, 1, 3):
            ring_x(e, n).start()

    def relay_x(e):
        rows = 64 if e else 128
        ring_x(e, 0).wait_recv()
        ring_x(e, 4).start()
        ring_x(e, 2).wait_recv()
        ring_x(e, 5).start()
        to_peer(near(e, -1), 0, rows)
        to_peer(near(e, 1), rows, rows)

    def finish_x(e):
        rows = 64 if e else 128
        for n, owner, lower in ((1, -1, 1), (3, 1, 0), (4, 2, 0), (5, 2, 1)):
            ring_x(e, n).wait_recv()
            to_peer(near(e, owner), lower * rows, rows)

    class RingY:
        def __init__(self, sh, src, first, rows, sem):
            self.sh, self.src, self.first, self.rows, self.sem = sh, src, first, rows, sem

        def copy(self, m):
            owner, lower, part, way = ((0, 0, 1, 1), (0, 0, 1, 3), (-1, 0, 2, 1), (1, 1, 2, 3))[m]
            size = self.rows // part
            ref = params.at[some(self.sh, self.first + lower * size, size), col(owner)]
            src = self.src if self.src is not None and m < 2 else ref
            return gather(src, ref, self.sem + min(m, 2), at_y(way))

        def launch(self):
            self.copy(0).start()
            self.copy(1).start()

        def relay(self):
            self.copy(0).wait_recv()
            self.copy(2).start()
            self.copy(1).wait_recv()
            self.copy(3).start()

        def finish(self):
            came_all(params.at[some(self.sh, self.first, self.rows), 0:128], pr.at[self.sem + 2])
            to_peer(self.sh, self.first, self.rows)

    keep_other = pltpu.make_async_copy(other_p, params.at[some(other, 0, HALF), col(0)], local.at[0])
    keep_other.start()

    for k in range(1, 4):
        piece_x(1, k, 0, HALF, 6).start()
    rings = [RingY(other, other_p, 0, HALF, 9)]
    rings += [RingY(near(1, -k), None, 0, HALF, 9 + 3 * k) for k in (1, 2, 3)]
    rings[0].launch()

    for n in range(4):
        own_block(c, y, n)
    came_all(gq.at[0, 0:3], gr.at[2])
    group_c.start()
    other_blocks()
    launch_x(0)
    for copy in keep(c, 1):
        copy.start()
    rest()
    keep_other.wait()
    rings[0].relay()
    for k in range(1, 4):
        piece_x(1, k, 0, HALF, 6).wait_recv()
        rings[k].launch()
    relay_x(0)
    for k in range(1, 4):
        rings[k].relay()
    rings[0].finish()
    finish_x(0)
    for k in range(1, 4):
        rings[k].finish()

    all_sent(11, gq.at[0])
    came_all(params.at[0:7 * HALF, :], kr.at[0])
    all_sent(12, params.at[0:27 * 64, :])
    all_sent(13, params.at[0:7 * HALF, :])
    for copy in keep(c, 1) + keep(1 - c, 6):
        copy.wait()
    for wait in left:
        wait()


def store(*refs):
    copies = [pltpu.make_async_copy(refs[n], refs[5 + n], refs[10].at[n]) for n in range(5)]
    for copy in copies[::-1]:
        copy.start()
    for copy in copies:
        copy.wait()


def shards(activations, out_grad, master, moment_one, moment_two, alive, step_count):
    hbm = pl.BlockSpec(memory_space=pl.ANY)
    dma = pltpu.SemaphoreType.DMA
    vm = pltpu.VMEM
    results = [((SH, KVW), F32)] * 4 + [((DW, KVW), BF16)]
    held = pl.pallas_call(
        kernel,
        out_shape=[vm(*r) for r in results],
        in_specs=[hbm] * 5 + [pl.BlockSpec(memory_space=pltpu.SMEM), pl.BlockSpec(memory_space=vm)],
        out_specs=[hbm] * 5,
        scratch_shapes=[
            vm((SH, KVW), F32), vm((SH, KVW), F32), vm((SH, KVW), F32), vm((SH, KVW), F32),
            vm((SH, KVW), BF16), vm((HALF, 128), BF16),
            vm((TOK, DW), BF16), vm((TOK, KVW), BF16),
            vm((SH, KVW), F32), vm((SH, KVW), F32), vm((SH, KVW), F32), vm((3, HALF, 128), F32),
            vm((8, SH, KVW), F32), vm((8, QR, KVW), I16), vm((8, QR, KVW), I16), vm((8, HALF, KVW), F32),
            vm((8, QR, KVW), I16), vm((8, QR, KVW), I16), vm((24, QR, 128), I16),
            vm((2, QR, KVW), I16), vm((2, 3, QR, 128), I16), vm((2, 3, QR, 128), I16),
            vm((HALF, KVW), F32), vm((2, HALF, 128), F32),
            vm((7, 80, 128), I16), vm((7, 80, 128), I16),
            vm((64, 128), F32), vm((2, 4, 4, 80, 128), I16), vm((4, 80, 128), I16),
            vm((8, 8, 128), F32), vm((16, 8, 128), F32), vm((2, 8, 128), F32),
            dma((12,)), dma((14,)), dma((8,)), dma((8,)), dma((2,)), dma((1,)), dma((1,)), dma((3,)), dma((4,)),
            dma((21,)), dma((1,)), dma((11,)),
        ],
        compiler_params=pltpu.CompilerParams(
            collective_id=0, has_side_effects=True, vmem_limit_bytes=50 * 2**20),
        name="reduce_update_gather",
    )(activations, out_grad, master, moment_one, moment_two, alive, step_count.reshape(1, 1))
    return tuple(pl.pallas_call(
        store,
        out_shape=[jax.ShapeDtypeStruct(*r) for r in results],
        in_specs=[hbm] * 5,
        out_specs=[hbm] * 5,
        scratch_shapes=[dma((5,))],
        compiler_params=pltpu.CompilerParams(vmem_limit_bytes=2**20),
        name="store_results",
    )(*(pltpu.with_memory_space_constraint(v, vm) for v in held)))


def solution(mesh):
    return jax.shard_map(
        shards,
        mesh=mesh,
        in_specs=(
            P(("replica", "shard"), None),
            P(("replica", "shard"), None),
            P("shard", None),
            P("shard", None),
            P("shard", None),
            P(),
            P(),
        ),
        out_specs=(P("shard", None), P("shard", None), P("shard", None), P("shard", None), P()),
        check_vma=False,
    )
```

```python
import functools

import jax
import jax.numpy as jnp
from jax import lax
from jax.experimental import pallas as pl
from jax.experimental.pallas import tpu as pltpu
from jax.sharding import PartitionSpec as P

DW = 4096
KVW = 512
TOK = 1024
SH = 512
HALF = 256
QR = HALF + 16
LEVELS = 32000.0
F32 = jnp.float32
BF16 = jnp.bfloat16
I16 = jnp.int16
MESH = pl.DeviceIdType.MESH


def place():
    r = lax.axis_index("replica")
    s = lax.axis_index("shard")
    return s // 2, r // 8, (s % 2) * 4 + (r // 2) % 4, r % 2


def dev(x, y, z, c):
    return ((y * 4 + z % 4) * 2 + c, x * 2 + z // 4)


def remote(src, dst, ssem, rsem, who):
    return pltpu.make_async_remote_copy(
        src_ref=src, dst_ref=dst, send_sem=ssem, recv_sem=rsem, device_id=who, device_id_type=MESH
    )


def turn(t):
    k = 3 - t % 4
    return k + (k // 2) * (5 - 2 * k)


def span(start, size):
    return pl.ds(pl.multiple_of(start, size), size)


def step_of(code):
    return jnp.exp2(code * 0.125)


def fold_max(acc, block):
    rows, cols = block.shape
    return jnp.maximum(acc, jnp.max(jnp.abs(block).reshape(rows // 8, 8, cols), axis=0))


def code_of(largest):
    top = jnp.max(largest, axis=0, keepdims=True)
    code = jnp.clip(jnp.ceil(8.0 * jnp.log2(jnp.maximum(top, 1e-37) * (1.0 / LEVELS))), -960.0, 960.0)
    return code, step_of(-code)


def quantized(block, inverse):
    return jnp.round(block * inverse).astype(jnp.int32).astype(I16)


def code_rows(code):
    return jnp.broadcast_to(code.astype(jnp.int32), (16, code.shape[1])).astype(I16)


def encode(read, q, rows, cols, chunk, largest):
    code, inverse = code_of(largest)

    @pl.loop(0, rows // chunk, unroll=True)
    def _(i):
        at = pl.multiple_of(i * chunk, chunk)
        q[pl.ds(at, chunk), :] = quantized(read(at), inverse)

    q[pl.ds(rows, 16), :] = code_rows(code)


def step_in(q, rows):
    return step_of(q[pl.ds(rows, 16), :].astype(jnp.int32).astype(F32)[0:1, :])


def decoded(q, at, chunk, step):
    return q[pl.ds(at, chunk), :].astype(jnp.int32).astype(F32) * step


def kernel(act, grad, master, m1, m2, alive, steps, clipped_h, master_h, m1_h, m2_h, params,
           clipped_o, master_o, m1_o, m2_o, near_p, other_p, a, b, w0, w1, w2, ow, g, pq, got, own, q1s, q1rx, q1ry, q2x, q2y, q2r, full, part, q3s, q3r, block, gq, oq,
           nz, nxy, nc, asem, sent, cr, s1r, s2r, s3r, orr, nr, gr, pr, kr, local):
    x, y, z, c = place()
    zh, zl = z // 4, z % 4
    peer = dev(x, y, z, 1 - c)
    shard = x * 2 + zh
    other = x * 2 + 1 - zh
    left = []

    def at_x(k):
        return dev((x + k) % 4, y, z, c)

    def at_y(k):
        return dev(x, (y + k) % 4, z, c)

    def at_z(k):
        return dev(x, y, (z + k) % 8, c)

    def at_zl(k, h):
        return dev(x, y, (zh if h else 1 - zh) * 4 + (zl + k) % 4, c)

    xy = [(i, j) for i in range(4) for j in range(4) if (i, j) != (0, 0)]

    def at_xy(k):
        return dev((x + xy[k][0]) % 4, (y + xy[k][1]) % 4, z, c)

    def a_copy(t):
        cols = span((((x + turn(t)) % 4) * 2 + jnp.where(t < 4, 1 - zh, zh)) * SH, SH)
        return pltpu.make_async_copy(act.at[:, cols], a.at[:, cols], asem.at[t])

    b_copy = pltpu.make_async_copy(grad, b, asem.at[8])
    b_copy.start()
    for t in range(2):
        a_copy(t).start()
    state = [pltpu.make_async_copy(src, dst, asem.at[9 + n]) for n, (src, dst) in
             enumerate(((master, w0), (m1, w1), (m2, w2)))]
    weight = alive[lax.axis_index("replica")].astype(F32)

    barrier = pltpu.get_barrier_semaphore()
    pl.semaphore_signal(barrier, inc=1, device_id=peer, device_id_type=MESH)
    for k in range(15):
        pl.semaphore_signal(barrier, inc=1, device_id=at_xy(k), device_id_type=MESH)
    for k in range(1, 8):
        pl.semaphore_signal(barrier, inc=1, device_id=at_z(k), device_id_type=MESH)

    b_copy.wait()
    def core_copy(t):
        return remote(pq.at[t], got.at[t], sent.at[0], cr.at[t], peer)

    def wait_for(t):
        a_copy(t).wait()

    def product(t):
        cols = span((((x + turn(t)) % 4) * 2 + jnp.where(t < 4, 1 - zh, zh)) * SH, SH)
        g[t] = lax.dot_general(a[:, cols], b[...], (((0,), (0,)), ((), ())), preferred_element_type=F32)

    def first_x(t):
        return remote(q1s.at[t], q1rx.at[t], sent.at[1], s1r.at[t], at_x(turn(t)))

    def first_y(t, j):
        return remote(q1s.at[t, :, span(((y + j + 1) % 4) * 128, 128)], q1ry.at[t * 3 + j], sent.at[1],
                      s1r.at[t], at_y(j + 1))

    def for_peer(t):
        largest = jnp.zeros((8, KVW), F32)
        for n in range(8):
            largest = fold_max(largest, g[t, span((1 - c) * HALF + n * 32, 32), :])
        code, inverse = code_of(largest * weight)
        inverse = inverse * weight
        for n in range(8):
            pq[t, n * 32:(n + 1) * 32, :] = quantized(g[t, span((1 - c) * HALF + n * 32, 32), :], inverse)
        pq[t, HALF:QR, :] = code_rows(code)

    def summed(t):
        largest = jnp.zeros((8, KVW), F32)
        step = step_in(got.at[t], HALF)
        for n in range(8):
            rows = span(c * HALF + n * 32, 32)
            total = g[t, rows, :] * weight + decoded(got.at[t], n * 32, 32, step)
            own[t, n * 32:(n + 1) * 32, :] = total
            largest = fold_max(largest, total)
        return largest

    def coded(t, largest):
        code, inverse = code_of(largest)
        for n in range(8):
            q1s[t, n * 32:(n + 1) * 32, :] = quantized(own[t, n * 32:(n + 1) * 32, :], inverse)
        q1s[t, HALF:QR, :] = code_rows(code)

    def send(t):
        @pl.when(jnp.logical_and(c == 0, t % 4 < 3))
        def _():
            first_x(t).start()

        @pl.when(c == 1)
        def _():
            for j in range(3):
                first_y(t, j).start()

    wait_for(0)
    for t in range(2, 8):
        a_copy(t).start()
    product(0)
    for_peer(0)
    pl.semaphore_wait(barrier, 23)
    core_copy(0).start()
    piece = (span(c * HALF, HALF), span(y * 128, 128))
    lend = [remote(src.at[piece[0], piece[1]], ow.at[n], sent.at[2], orr.at[0], at_z(4)) for n, src in
            enumerate((master, m1, m2))]
    for copy in lend:
        copy.start()

    @pl.loop(1, 8)
    def _(t):
        wait_for(t)
        product(t)
        for_peer(t)
        core_copy(t).start()
        core_copy(t - 1).wait_recv()
        coded(t - 1, summed(t - 1))
        send(t - 1)

    core_copy(7).wait_recv()
    coded(7, summed(7))
    send(7)
    for copy in state:
        copy.start()
    def all_sent(sem, ref):
        left.append(remote(ref, ref, sent.at[sem], sent.at[sem], peer).wait_send)

    def came_all(ref, sem):
        remote(ref, ref, sent.at[0], sem, peer).wait_recv()

    all_sent(0, pq)
    all_sent(1, q1s.at[0:6])
    all_sent(2, ow)

    def second_y(h, j):
        return remote(q2x.at[h, :, span(((y + j + 1) % 4) * 128, 128)], q2r.at[h, j], sent.at[3],
                      s2r.at[h], at_y(j + 1))

    def second_x(h, i):
        return remote(q2y.at[h, i], q2r.at[h, i], sent.at[3], s2r.at[h], at_x(turn(i)))

    def first_sums(h):
        @pl.when(c == 0)
        def _():
            for i in range(3):
                first_x(h * 4 + i).wait_recv()
            step = [step_in(q1rx.at[h * 4 + i], HALF) for i in range(3)]

            def add(n, acc):
                at = pl.multiple_of(n * 32, 32)
                total = own[h * 4 + 3, pl.ds(at, 32), :]
                for i in range(3):
                    total += decoded(q1rx.at[h * 4 + i], at, 32, step[i])
                full[pl.ds(at, 32), :] = total
                return fold_max(acc, total)

            largest = lax.fori_loop(0, HALF // 32, add, jnp.zeros((8, KVW), F32))
            encode(lambda at: full[pl.ds(at, 32), :], q2x.at[h], HALF, KVW, 32, largest)
            for j in range(3):
                second_y(h, j).start()
            part[h] = full[:, span(y * 128, 128)]

        @pl.when(c == 1)
        def _():
            @pl.loop(0, 4)
            def _(i):
                t = h * 4 + i
                came_all(q1ry.at[pl.ds(t * 3, 3)], s1r.at[t])
                step = [step_in(q1ry.at[t * 3 + j], HALF) for j in range(3)]

                def add(n, acc):
                    at = pl.multiple_of(n * 128, 128)
                    total = own[t, pl.ds(at, 128), span(y * 128, 128)]
                    for j in range(3):
                        total += decoded(q1ry.at[t * 3 + j], at, 128, step[j])
                    part[h, pl.ds(at, 128), :] = total
                    return fold_max(acc, total)

                largest = lax.fori_loop(0, 2, add, jnp.zeros((8, 128), F32))

                @pl.when(i < 3)
                def _():
                    encode(lambda at: part[h, pl.ds(at, 128), :], q2y.at[h, i], HALF, 128, 128, largest)
                    second_x(h, i).start()

    def third(h, k):
        n = h * 3 + k
        return remote(q3s.at[n], q3r.at[n], sent.at[4], s3r.at[0], at_zl(k, h))

    def second_sums(h):
        came_all(q2r.at[h], s2r.at[h])
        step = [step_in(q2r.at[h, j], HALF) for j in range(3)]
        largest = jnp.zeros((8, 128), F32)
        for n in range(4):
            at = n * 64
            total = part[h, at:at + 64, :]
            for j in range(3):
                total += decoded(q2r.at[h, j], at, 64, step[j])
            part[h, at:at + 64, :] = total
            largest = fold_max(largest, total)
        code, inverse = code_of(largest)
        for k in range(h, 4):
            q3s[h * 3 + k, 0:64, :] = quantized(part[h, span(((zl + k) % 4) * 64, 64), :], inverse)
            q3s[h * 3 + k, 64:80, :] = code_rows(code)
        for k in range(h, 4):
            third(h, k).start()

    all_sent(3, q2r)
    all_sent(4, q3s)
    first_sums(0)
    second_sums(0)
    first_sums(1)
    second_sums(1)
    total = part[1, span(zl * 64, 64), :]
    came_all(q3r, s3r.at[0])
    for n in range(7):
        total += decoded(q3r.at[n], 0, 64, step_in(q3r.at[n], 64))

    mine = gq.at[c, y, zl]
    def tell_z(k):
        return remote(nz.at[z], nz.at[z], sent.at[5], nr.at[0], at_z(k))

    def tell_xy(k):
        slot = nxy.at[x * 4 + y]
        return remote(slot, slot, sent.at[6], nr.at[1], at_xy(k))

    tell_c = remote(nc.at[c], nc.at[c], sent.at[7], nr.at[2], peer)

    def group_z(k):
        return remote(mine, mine, sent.at[8], gr.at[0], at_zl(k, 1))

    def cross_z(k):
        return remote(mine, oq.at[zl], sent.at[9], gr.at[1], at_zl(k, 0))

    def group_y(k):
        return remote(gq.at[c, y], gq.at[c, y], sent.at[10], gr.at[2], at_y(k))

    group_c = remote(gq.at[c], gq.at[c], sent.at[11], gr.at[3], peer)

    nxy[x * 4 + y] = jnp.sum((total * total).reshape(8, 8, 128), axis=0)
    for k in range(15):
        tell_xy(k).start()
    encode(lambda at: total, mine, 64, 128, 64, fold_max(jnp.zeros((8, 128), F32), total))
    for k in range(1, 4):
        group_z(k).start()
    came_all(nxy.at[0:15], nr.at[1])
    nz[z] = jnp.sum(nxy[...], axis=0)
    for k in range(1, 8):
        tell_z(k).start()
    for k in range(4):
        cross_z(k).start()
    came_all(gq.at[0, 0, 0:3], gr.at[0])

    for k in range(1, 4):
        group_y(k).start()
    came_all(nz.at[0:7], nr.at[0])
    nc[c] = jnp.sum(nz[...], axis=0)
    tell_c.start()
    for copy in state:
        copy.wait()
    came_all(ow, orr.at[0])
    came_all(oq, gr.at[1])
    tell_c.wait_recv()
    square = jnp.sum(nc[0] + nc[1], keepdims=True)
    factor = jnp.minimum(1.0, jnp.sqrt(F32(DW * KVW)) / jnp.sqrt(square + 1e-06))

    all_sent(5, nz.at[0:7])
    all_sent(6, nxy.at[0:15])
    all_sent(7, nc.at[0])
    all_sent(8, gq.at[0, 0, 0:3])
    all_sent(9, oq)
    all_sent(10, gq.at[0, 0:3])

    done = jnp.full((1, 128), steps[0].astype(F32))
    correct1 = 1.0 / (1.0 - jnp.exp(done * jnp.log(F32(0.9))))
    correct2 = 1.0 / (1.0 - jnp.exp(done * jnp.log(F32(0.95))))

    def adam(q, old, one, two):
        clipped = decoded(q, 0, 64, step_in(q, 64)) * factor
        one = 0.9 * one + 0.1 * clipped
        two = 0.95 * two + 0.05 * clipped * clipped
        new = old - 0.01 * ((one * correct1) / (jnp.sqrt(two * correct2) + 1e-08) + 0.1 * old)
        return clipped, new, one, two

    def col(k):
        return span(((y + k + 4) % 4) * 128, 128)

    for n in range(4):
        rows = pl.ds(n * 64, 64)
        new = adam(oq.at[n], ow[0, rows, :], ow[1, rows, :], ow[2, rows, :])[1]
        other_p[n * 64:(n + 1) * 64, :] = new.astype(BF16)

    rows_c = span(c * HALF, HALF)

    def own_block(cc, yy, zz):
        rows = span(cc * HALF + zz * 64, 64)
        cols = span(yy * 128, 128)
        clipped, new, one, two = adam(gq.at[cc, yy, zz], w0[rows, cols], w1[rows, cols], w2[rows, cols])
        clipped_o[rows, cols] = clipped
        master_o[rows, cols] = new
        m1_o[rows, cols] = one
        m2_o[rows, cols] = two
        near_p[rows, cols] = new.astype(BF16)

    def other_blocks():
        @pl.loop(0, 12, unroll=4)
        def _(n):
            own_block(c, (y + 1 + n // 4) % 4, n % 4)

    outs = [(clipped_o, clipped_h), (master_o, master_h), (m1_o, m1_h), (m2_o, m2_h)]

    def keep(cc, n):
        rows = span(cc * HALF, HALF)
        copies = [pltpu.make_async_copy(src.at[rows, :], dst.at[rows, :], local.at[n + i]) for i, (src, dst) in enumerate(outs)]
        there = params.at[span(shard * SH + cc * HALF, HALF), :]
        return copies + [pltpu.make_async_copy(near_p.at[rows, :], there, local.at[n + 4])]

    def rest():
        group_c.wait_recv()

        @pl.loop(0, 16, unroll=4)
        def _(n):
            own_block(1 - c, n // 4, n % 4)

        for copy in keep(1 - c, 6):
            copy.start()

    def near(e, k):
        return ((x + k + 4) % 4) * 2 + (1 - zh if e else zh)

    def some(sh, first, rows):
        return pl.ds(pl.multiple_of(sh * SH + c * HALF + first, 64), rows)

    def to_peer(sh, first, rows):
        ref = params.at[some(sh, first, rows), :]
        remote(ref, ref, sent.at[13], kr.at[0], peer).start()

    def gather(src, dst, sem, who):
        return remote(src, dst, sent.at[12], pr.at[sem], who)

    def piece_x(e, k, first, rows, sem):
        src = other_p.at[first:first + rows, :] if e else near_p.at[some(0, first, rows), col(0)]
        return gather(src, params.at[some(near(e, 0), first, rows), col(0)], sem + k - 1, at_x(k))

    def ring_x(e, n):
        owner, lower, way = ((0, 0, 1), (0, 1, 1), (0, 1, 3), (0, 0, 3), (-1, 0, 1), (1, 1, 3))[n]
        rows = 64 if e else 128
        ref = params.at[some(near(e, owner), lower * rows, rows), :]
        src = near_p.at[some(0, lower * rows, rows), :] if e == 0 and n < 4 else ref
        return gather(src, ref, e * 6 + n, at_x(way))

    def launch_x(e):
        for n in (0, 2, 1, 3):
            ring_x(e, n).start()

    def relay_x(e):
        rows = 64 if e else 128
        ring_x(e, 0).wait_recv()
        ring_x(e, 4).start()
        ring_x(e, 2).wait_recv()
        ring_x(e, 5).start()
        to_peer(near(e, -1), 0, rows)
        to_peer(near(e, 1), rows, rows)

    def finish_x(e, which):
        rows = 64 if e else 128
        for n, owner, lower in [((1, -1, 1), (3, 1, 0), (4, 2, 0), (5, 2, 1))[i] for i in which]:
            ring_x(e, n).wait_recv()
            to_peer(near(e, owner), lower * rows, rows)

    class RingY:
        def __init__(self, sh, src, first, rows, sem):
            self.sh, self.src, self.first, self.rows, self.sem = sh, src, first, rows, sem

        def copy(self, m):
            owner, lower, part, way = ((0, 0, 1, 1), (0, 0, 1, 3), (-1, 0, 2, 1), (1, 1, 2, 3))[m]
            size = self.rows // part
            ref = params.at[some(self.sh, self.first + lower * size, size), col(owner)]
            src = self.src if self.src is not None and m < 2 else ref
            return gather(src, ref, self.sem + min(m, 2), at_y(way))

        def launch(self):
            self.copy(0).start()
            self.copy(1).start()

        def relay(self):
            self.copy(0).wait_recv()
            self.copy(2).start()
            self.copy(1).wait_recv()
            self.copy(3).start()

        def finish(self):
            came_all(params.at[some(self.sh, self.first, self.rows), 0:128], pr.at[self.sem + 2])
            to_peer(self.sh, self.first, self.rows)

    keep_other = pltpu.make_async_copy(other_p, params.at[some(other, 0, HALF), col(0)], local.at[0])
    keep_other.start()

    for k in range(1, 4):
        piece_x(1, k, 0, HALF, 6).start()
    rings = [RingY(other, other_p, 0, HALF, 9)]
    rings += [RingY(near(1, -k), None, 0, HALF, 9 + 3 * k) for k in (1, 2, 3)]
    rings[0].launch()

    for n in range(4):
        own_block(c, y, n)
    came_all(gq.at[0, 0:3], gr.at[2])
    group_c.start()
    other_blocks()
    launch_x(0)
    for copy in keep(c, 1):
        copy.start()
    rest()
    keep_other.wait()
    rings[0].relay()
    for k in (1, 3, 2):
        piece_x(1, k, 0, HALF, 6).wait_recv()
        rings[k].launch()
    relay_x(0)
    rings[0].finish()
    for k in (1, 3, 2):
        rings[k].relay()
    finish_x(0, (0, 1))
    rings[1].finish()
    rings[3].finish()
    finish_x(0, (2, 3))
    rings[2].finish()

    all_sent(11, gq.at[0])
    came_all(params.at[0:7 * HALF, :], kr.at[0])
    all_sent(12, params.at[0:27 * 64, :])
    all_sent(13, params.at[0:7 * HALF, :])
    for copy in keep(c, 1) + keep(1 - c, 6):
        copy.wait()
    for wait in left:
        wait()


def store(*refs):
    copies = [pltpu.make_async_copy(refs[n], refs[5 + n], refs[10].at[n]) for n in range(5)]
    for copy in copies[::-1]:
        copy.start()
    for copy in copies:
        copy.wait()


def shards(activations, out_grad, master, moment_one, moment_two, alive, step_count):
    hbm = pl.BlockSpec(memory_space=pl.ANY)
    dma = pltpu.SemaphoreType.DMA
    vm = pltpu.VMEM
    results = [((SH, KVW), F32)] * 4 + [((DW, KVW), BF16)]
    held = pl.pallas_call(
        kernel,
        out_shape=[vm(*r) for r in results],
        in_specs=[hbm] * 5 + [pl.BlockSpec(memory_space=pltpu.SMEM)] * 2,
        out_specs=[hbm] * 5,
        scratch_shapes=[
            vm((SH, KVW), F32), vm((SH, KVW), F32), vm((SH, KVW), F32), vm((SH, KVW), F32),
            vm((SH, KVW), BF16), vm((HALF, 128), BF16),
            vm((TOK, DW), BF16), vm((TOK, KVW), BF16),
            vm((SH, KVW), F32), vm((SH, KVW), F32), vm((SH, KVW), F32), vm((3, HALF, 128), F32),
            vm((8, SH, KVW), F32), vm((8, QR, KVW), I16), vm((8, QR, KVW), I16), vm((8, HALF, KVW), F32),
            vm((8, QR, KVW), I16), vm((8, QR, KVW), I16), vm((24, QR, 128), I16),
            vm((2, QR, KVW), I16), vm((2, 3, QR, 128), I16), vm((2, 3, QR, 128), I16),
            vm((HALF, KVW), F32), vm((2, HALF, 128), F32),
            vm((7, 80, 128), I16), vm((7, 80, 128), I16),
            vm((64, 128), F32), vm((2, 4, 4, 80, 128), I16), vm((4, 80, 128), I16),
            vm((8, 8, 128), F32), vm((16, 8, 128), F32), vm((2, 8, 128), F32),
            dma((12,)), dma((14,)), dma((8,)), dma((8,)), dma((2,)), dma((1,)), dma((1,)), dma((3,)), dma((4,)),
            dma((21,)), dma((1,)), dma((11,)),
        ],
        compiler_params=pltpu.CompilerParams(
            collective_id=0, has_side_effects=True, vmem_limit_bytes=50 * 2**20),
        name="reduce_update_gather",
    )(activations, out_grad, master, moment_one, moment_two, alive, step_count)
    return tuple(pl.pallas_call(
        store,
        out_shape=[jax.ShapeDtypeStruct(*r) for r in results],
        in_specs=[hbm] * 5,
        out_specs=[hbm] * 5,
        scratch_shapes=[dma((5,))],
        compiler_params=pltpu.CompilerParams(vmem_limit_bytes=2**20),
        name="store_results",
    )(*(pltpu.with_memory_space_constraint(v, vm) for v in held)))


def solution(mesh):
    return jax.shard_map(
        shards,
        mesh=mesh,
        in_specs=(
            P(("replica", "shard"), None),
            P(("replica", "shard"), None),
            P("shard", None),
            P("shard", None),
            P("shard", None),
            P(),
            P(),
        ),
        out_specs=(P("shard", None), P("shard", None), P("shard", None), P("shard", None), P()),
        check_vma=False,
    )
```

```python
import functools

import jax
import jax.numpy as jnp
from jax import lax
from jax.experimental import pallas as pl
from jax.experimental.pallas import tpu as pltpu
from jax.sharding import PartitionSpec as P

DW = 4096
KVW = 512
TOK = 1024
SH = 512
HALF = 256
QR = HALF + 16
LEVELS = 32000.0
F32 = jnp.float32
BF16 = jnp.bfloat16
I16 = jnp.int16
MESH = pl.DeviceIdType.MESH


def place():
    r = lax.axis_index("replica")
    s = lax.axis_index("shard")
    return s // 2, r // 8, (s % 2) * 4 + (r // 2) % 4, r % 2


def dev(x, y, z, c):
    return ((y * 4 + z % 4) * 2 + c, x * 2 + z // 4)


def remote(src, dst, ssem, rsem, who):
    return pltpu.make_async_remote_copy(
        src_ref=src, dst_ref=dst, send_sem=ssem, recv_sem=rsem, device_id=who, device_id_type=MESH
    )


def turn(t):
    k = 3 - t % 4
    return k + (k // 2) * (5 - 2 * k)


def span(start, size):
    return pl.ds(pl.multiple_of(start, size), size)


def step_of(code):
    return jnp.exp2(code * 0.125)


def fold_max(acc, block):
    rows, cols = block.shape
    return jnp.maximum(acc, jnp.max(jnp.abs(block).reshape(rows // 8, 8, cols), axis=0))


def code_of(largest):
    top = jnp.max(largest, axis=0, keepdims=True)
    code = jnp.clip(jnp.ceil(8.0 * jnp.log2(jnp.maximum(top, 1e-37) * (1.0 / LEVELS))), -960.0, 960.0)
    return code, step_of(-code)


def quantized(block, inverse):
    return jnp.round(block * inverse).astype(jnp.int32).astype(I16)


def code_rows(code):
    return jnp.broadcast_to(code.astype(jnp.int32), (16, code.shape[1])).astype(I16)


def encode(read, q, rows, cols, chunk, largest):
    code, inverse = code_of(largest)

    @pl.loop(0, rows // chunk, unroll=True)
    def _(i):
        at = pl.multiple_of(i * chunk, chunk)
        q[pl.ds(at, chunk), :] = quantized(read(at), inverse)

    q[pl.ds(rows, 16), :] = code_rows(code)


def step_in(q, rows):
    return step_of(q[pl.ds(rows, 16), :].astype(jnp.int32).astype(F32)[0:1, :])


def decoded(q, at, chunk, step):
    return q[pl.ds(at, chunk), :].astype(jnp.int32).astype(F32) * step


def kernel(act, grad, master, m1, m2, alive_h, steps, clipped_h, master_h, m1_h, m2_h, params,
           clipped_o, master_o, m1_o, m2_o, near_p, other_p, a, b, w0, w1, w2, ow, g, pq, got, own, q1s, q1rx, q1ry, q2x, q2y, q2r, full, part, q3s, q3r, block, gq, oq,
           nz, nxy, nc, alive, asem, sent, cr, s1r, s2r, s3r, orr, nr, gr, pr, kr, local):
    x, y, z, c = place()
    zh, zl = z // 4, z % 4
    peer = dev(x, y, z, 1 - c)
    shard = x * 2 + zh
    other = x * 2 + 1 - zh
    left = []

    def at_x(k):
        return dev((x + k) % 4, y, z, c)

    def at_y(k):
        return dev(x, (y + k) % 4, z, c)

    def at_z(k):
        return dev(x, y, (z + k) % 8, c)

    def at_zl(k, h):
        return dev(x, y, (zh if h else 1 - zh) * 4 + (zl + k) % 4, c)

    xy = [(i, j) for i in range(4) for j in range(4) if (i, j) != (0, 0)]

    def at_xy(k):
        return dev((x + xy[k][0]) % 4, (y + xy[k][1]) % 4, z, c)

    def a_copy(t):
        cols = span((((x + turn(t)) % 4) * 2 + jnp.where(t < 4, 1 - zh, zh)) * SH, SH)
        return pltpu.make_async_copy(act.at[:, cols], a.at[:, cols], asem.at[t])

    b_copy = pltpu.make_async_copy(grad, b, asem.at[8])
    alive_copy = pltpu.make_async_copy(alive_h, alive, asem.at[12])
    b_copy.start()
    alive_copy.start()
    for t in range(2):
        a_copy(t).start()
    state = [pltpu.make_async_copy(src, dst, asem.at[9 + n]) for n, (src, dst) in
             enumerate(((master, w0), (m1, w1), (m2, w2)))]

    barrier = pltpu.get_barrier_semaphore()
    pl.semaphore_signal(barrier, inc=1, device_id=peer, device_id_type=MESH)
    for k in range(15):
        pl.semaphore_signal(barrier, inc=1, device_id=at_xy(k), device_id_type=MESH)
    for k in range(1, 8):
        pl.semaphore_signal(barrier, inc=1, device_id=at_z(k), device_id_type=MESH)

    b_copy.wait()
    alive_copy.wait()
    weight = alive[lax.axis_index("replica")].astype(F32)
    def core_copy(t):
        return remote(pq.at[t], got.at[t], sent.at[0], cr.at[t], peer)

    def wait_for(t):
        a_copy(t).wait()

    def product(t):
        cols = span((((x + turn(t)) % 4) * 2 + jnp.where(t < 4, 1 - zh, zh)) * SH, SH)
        g[t] = lax.dot_general(a[:, cols], b[...], (((0,), (0,)), ((), ())), preferred_element_type=F32)

    def first_x(t):
        return remote(q1s.at[t], q1rx.at[t], sent.at[1], s1r.at[t], at_x(turn(t)))

    def first_y(t, j):
        return remote(q1s.at[t, :, span(((y + j + 1) % 4) * 128, 128)], q1ry.at[t * 3 + j], sent.at[1],
                      s1r.at[t], at_y(j + 1))

    def for_peer(t):
        largest = jnp.zeros((8, KVW), F32)
        for n in range(8):
            largest = fold_max(largest, g[t, span((1 - c) * HALF + n * 32, 32), :])
        code, inverse = code_of(largest * weight)
        inverse = inverse * weight
        for n in range(8):
            pq[t, n * 32:(n + 1) * 32, :] = quantized(g[t, span((1 - c) * HALF + n * 32, 32), :], inverse)
        pq[t, HALF:QR, :] = code_rows(code)

    def summed(t):
        largest = jnp.zeros((8, KVW), F32)
        step = step_in(got.at[t], HALF)
        for n in range(8):
            rows = span(c * HALF + n * 32, 32)
            total = g[t, rows, :] * weight + decoded(got.at[t], n * 32, 32, step)
            own[t, n * 32:(n + 1) * 32, :] = total
            largest = fold_max(largest, total)
        return largest

    def coded(t, largest):
        code, inverse = code_of(largest)
        for n in range(8):
            q1s[t, n * 32:(n + 1) * 32, :] = quantized(own[t, n * 32:(n + 1) * 32, :], inverse)
        q1s[t, HALF:QR, :] = code_rows(code)

    def send(t):
        @pl.when(jnp.logical_and(c == 0, t % 4 < 3))
        def _():
            first_x(t).start()

        @pl.when(c == 1)
        def _():
            for j in range(3):
                first_y(t, j).start()

    wait_for(0)
    for t in range(2, 8):
        a_copy(t).start()
    product(0)
    for_peer(0)
    pl.semaphore_wait(barrier, 23)
    core_copy(0).start()
    piece = (span(c * HALF, HALF), span(y * 128, 128))
    lend = [remote(src.at[piece[0], piece[1]], ow.at[n], sent.at[2], orr.at[0], at_z(4)) for n, src in
            enumerate((master, m1, m2))]
    for copy in lend:
        copy.start()

    @pl.loop(1, 8)
    def _(t):
        wait_for(t)
        product(t)
        for_peer(t)
        core_copy(t).start()
        core_copy(t - 1).wait_recv()
        coded(t - 1, summed(t - 1))
        send(t - 1)

    core_copy(7).wait_recv()
    coded(7, summed(7))
    send(7)
    for copy in state:
        copy.start()
    def all_sent(sem, ref):
        left.append(remote(ref, ref, sent.at[sem], sent.at[sem], peer).wait_send)

    def came_all(ref, sem):
        remote(ref, ref, sent.at[0], sem, peer).wait_recv()

    all_sent(0, pq)
    all_sent(1, q1s.at[0:6])
    all_sent(2, ow)

    def second_y(h, j):
        return remote(q2x.at[h, :, span(((y + j + 1) % 4) * 128, 128)], q2r.at[h, j], sent.at[3],
                      s2r.at[h], at_y(j + 1))

    def second_x(h, i):
        return remote(q2y.at[h, i], q2r.at[h, i], sent.at[3], s2r.at[h], at_x(turn(i)))

    def first_sums(h):
        @pl.when(c == 0)
        def _():
            for i in range(3):
                first_x(h * 4 + i).wait_recv()
            step = [step_in(q1rx.at[h * 4 + i], HALF) for i in range(3)]

            def add(n, acc):
                at = pl.multiple_of(n * 32, 32)
                total = own[h * 4 + 3, pl.ds(at, 32), :]
                for i in range(3):
                    total += decoded(q1rx.at[h * 4 + i], at, 32, step[i])
                full[pl.ds(at, 32), :] = total
                return fold_max(acc, total)

            largest = lax.fori_loop(0, HALF // 32, add, jnp.zeros((8, KVW), F32))
            encode(lambda at: full[pl.ds(at, 32), :], q2x.at[h], HALF, KVW, 32, largest)
            for j in range(3):
                second_y(h, j).start()
            part[h] = full[:, span(y * 128, 128)]

        @pl.when(c == 1)
        def _():
            @pl.loop(0, 4)
            def _(i):
                t = h * 4 + i
                came_all(q1ry.at[pl.ds(t * 3, 3)], s1r.at[t])
                step = [step_in(q1ry.at[t * 3 + j], HALF) for j in range(3)]

                def add(n, acc):
                    at = pl.multiple_of(n * 128, 128)
                    total = own[t, pl.ds(at, 128), span(y * 128, 128)]
                    for j in range(3):
                        total += decoded(q1ry.at[t * 3 + j], at, 128, step[j])
                    part[h, pl.ds(at, 128), :] = total
                    return fold_max(acc, total)

                largest = lax.fori_loop(0, 2, add, jnp.zeros((8, 128), F32))

                @pl.when(i < 3)
                def _():
                    encode(lambda at: part[h, pl.ds(at, 128), :], q2y.at[h, i], HALF, 128, 128, largest)
                    second_x(h, i).start()

    def third(h, k):
        n = h * 3 + k
        return remote(q3s.at[n], q3r.at[n], sent.at[4], s3r.at[0], at_zl(k, h))

    def second_sums(h):
        came_all(q2r.at[h], s2r.at[h])
        step = [step_in(q2r.at[h, j], HALF) for j in range(3)]
        largest = jnp.zeros((8, 128), F32)
        for n in range(4):
            at = n * 64
            total = part[h, at:at + 64, :]
            for j in range(3):
                total += decoded(q2r.at[h, j], at, 64, step[j])
            part[h, at:at + 64, :] = total
            largest = fold_max(largest, total)
        code, inverse = code_of(largest)
        for k in range(h, 4):
            q3s[h * 3 + k, 0:64, :] = quantized(part[h, span(((zl + k) % 4) * 64, 64), :], inverse)
            q3s[h * 3 + k, 64:80, :] = code_rows(code)
        for k in range(h, 4):
            third(h, k).start()

    all_sent(3, q2r)
    all_sent(4, q3s)
    first_sums(0)
    second_sums(0)
    first_sums(1)
    second_sums(1)
    total = part[1, span(zl * 64, 64), :]
    came_all(q3r, s3r.at[0])
    for n in range(7):
        total += decoded(q3r.at[n], 0, 64, step_in(q3r.at[n], 64))

    mine = gq.at[c, y, zl]
    def tell_z(k):
        return remote(nz.at[z], nz.at[z], sent.at[5], nr.at[0], at_z(k))

    def tell_xy(k):
        slot = nxy.at[x * 4 + y]
        return remote(slot, slot, sent.at[6], nr.at[1], at_xy(k))

    tell_c = remote(nc.at[c], nc.at[c], sent.at[7], nr.at[2], peer)

    def group_z(k):
        return remote(mine, mine, sent.at[8], gr.at[0], at_zl(k, 1))

    def cross_z(k):
        return remote(mine, oq.at[zl], sent.at[9], gr.at[1], at_zl(k, 0))

    def group_y(k):
        return remote(gq.at[c, y], gq.at[c, y], sent.at[10], gr.at[2], at_y(k))

    group_c = remote(gq.at[c], gq.at[c], sent.at[11], gr.at[3], peer)

    nxy[x * 4 + y] = jnp.sum((total * total).reshape(8, 8, 128), axis=0)
    for k in range(15):
        tell_xy(k).start()
    encode(lambda at: total, mine, 64, 128, 64, fold_max(jnp.zeros((8, 128), F32), total))
    for k in range(1, 4):
        group_z(k).start()
    came_all(nxy.at[0:15], nr.at[1])
    nz[z] = jnp.sum(nxy[...], axis=0)
    for k in range(1, 8):
        tell_z(k).start()
    for k in range(4):
        cross_z(k).start()
    came_all(gq.at[0, 0, 0:3], gr.at[0])

    for k in range(1, 4):
        group_y(k).start()
    came_all(nz.at[0:7], nr.at[0])
    nc[c] = jnp.sum(nz[...], axis=0)
    tell_c.start()
    for copy in state:
        copy.wait()
    came_all(ow, orr.at[0])
    came_all(oq, gr.at[1])
    tell_c.wait_recv()
    square = jnp.sum(nc[0] + nc[1], keepdims=True)
    factor = jnp.minimum(1.0, jnp.sqrt(F32(DW * KVW)) / jnp.sqrt(square + 1e-06))

    all_sent(5, nz.at[0:7])
    all_sent(6, nxy.at[0:15])
    all_sent(7, nc.at[0])
    all_sent(8, gq.at[0, 0, 0:3])
    all_sent(9, oq)
    all_sent(10, gq.at[0, 0:3])

    done = jnp.full((1, 128), steps[0].astype(F32))
    correct1 = 1.0 / (1.0 - jnp.exp(done * jnp.log(F32(0.9))))
    correct2 = 1.0 / (1.0 - jnp.exp(done * jnp.log(F32(0.95))))

    def adam(q, old, one, two):
        clipped = decoded(q, 0, 64, step_in(q, 64)) * factor
        one = 0.9 * one + 0.1 * clipped
        two = 0.95 * two + 0.05 * clipped * clipped
        new = old - 0.01 * ((one * correct1) / (jnp.sqrt(two * correct2) + 1e-08) + 0.1 * old)
        return clipped, new, one, two

    def col(k):
        return span(((y + k + 4) % 4) * 128, 128)

    for n in range(4):
        rows = pl.ds(n * 64, 64)
        new = adam(oq.at[n], ow[0, rows, :], ow[1, rows, :], ow[2, rows, :])[1]
        other_p[n * 64:(n + 1) * 64, :] = new.astype(BF16)

    rows_c = span(c * HALF, HALF)

    def own_block(cc, yy, zz):
        rows = span(cc * HALF + zz * 64, 64)
        cols = span(yy * 128, 128)
        clipped, new, one, two = adam(gq.at[cc, yy, zz], w0[rows, cols], w1[rows, cols], w2[rows, cols])
        clipped_o[rows, cols] = clipped
        master_o[rows, cols] = new
        m1_o[rows, cols] = one
        m2_o[rows, cols] = two
        near_p[rows, cols] = new.astype(BF16)

    def other_blocks():
        @pl.loop(0, 12, unroll=4)
        def _(n):
            own_block(c, (y + 1 + n // 4) % 4, n % 4)

    outs = [(clipped_o, clipped_h), (master_o, master_h), (m1_o, m1_h), (m2_o, m2_h)]

    def keep(cc, n):
        rows = span(cc * HALF, HALF)
        copies = [pltpu.make_async_copy(src.at[rows, :], dst.at[rows, :], local.at[n + i]) for i, (src, dst) in enumerate(outs)]
        there = params.at[span(shard * SH + cc * HALF, HALF), :]
        return copies + [pltpu.make_async_copy(near_p.at[rows, :], there, local.at[n + 4])]

    def rest():
        group_c.wait_recv()

        @pl.loop(0, 16, unroll=4)
        def _(n):
            own_block(1 - c, n // 4, n % 4)

        for copy in keep(1 - c, 6):
            copy.start()

    def near(e, k):
        return ((x + k + 4) % 4) * 2 + (1 - zh if e else zh)

    def some(sh, first, rows):
        return pl.ds(pl.multiple_of(sh * SH + c * HALF + first, 64), rows)

    def to_peer(sh, first, rows):
        ref = params.at[some(sh, first, rows), :]
        remote(ref, ref, sent.at[13], kr.at[0], peer).start()

    def gather(src, dst, sem, who):
        return remote(src, dst, sent.at[12], pr.at[sem], who)

    def piece_x(e, k, first, rows, sem):
        src = other_p.at[first:first + rows, :] if e else near_p.at[some(0, first, rows), col(0)]
        return gather(src, params.at[some(near(e, 0), first, rows), col(0)], sem + k - 1, at_x(k))

    def ring_x(e, n):
        owner, lower, way = ((0, 0, 1), (0, 1, 1), (0, 1, 3), (0, 0, 3), (-1, 0, 1), (1, 1, 3))[n]
        rows = 64 if e else 128
        ref = params.at[some(near(e, owner), lower * rows, rows), :]
        src = near_p.at[some(0, lower * rows, rows), :] if e == 0 and n < 4 else ref
        return gather(src, ref, e * 6 + n, at_x(way))

    def launch_x(e):
        for n in (0, 2, 1, 3):
            ring_x(e, n).start()

    def relay_x(e):
        rows = 64 if e else 128
        ring_x(e, 0).wait_recv()
        ring_x(e, 4).start()
        ring_x(e, 2).wait_recv()
        ring_x(e, 5).start()
        to_peer(near(e, -1), 0, rows)
        to_peer(near(e, 1), rows, rows)

    def finish_x(e, which):
        rows = 64 if e else 128
        for n, owner, lower in [((1, -1, 1), (3, 1, 0), (4, 2, 0), (5, 2, 1))[i] for i in which]:
            ring_x(e, n).wait_recv()
            to_peer(near(e, owner), lower * rows, rows)

    class RingY:
        def __init__(self, sh, src, first, rows, sem):
            self.sh, self.src, self.first, self.rows, self.sem = sh, src, first, rows, sem

        def copy(self, m):
            owner, lower, part, way = ((0, 0, 1, 1), (0, 0, 1, 3), (-1, 0, 2, 1), (1, 1, 2, 3))[m]
            size = self.rows // part
            ref = params.at[some(self.sh, self.first + lower * size, size), col(owner)]
            src = self.src if self.src is not None and m < 2 else ref
            return gather(src, ref, self.sem + min(m, 2), at_y(way))

        def launch(self):
            self.copy(0).start()
            self.copy(1).start()

        def relay(self):
            self.copy(0).wait_recv()
            self.copy(2).start()
            self.copy(1).wait_recv()
            self.copy(3).start()

        def finish(self):
            came_all(params.at[some(self.sh, self.first, self.rows), 0:128], pr.at[self.sem + 2])
            to_peer(self.sh, self.first, self.rows)

    keep_other = pltpu.make_async_copy(other_p, params.at[some(other, 0, HALF), col(0)], local.at[0])
    keep_other.start()

    for k in range(1, 4):
        piece_x(1, k, 0, HALF, 6).start()
    rings = [RingY(other, other_p, 0, HALF, 9)]
    rings += [RingY(near(1, -k), None, 0, HALF, 9 + 3 * k) for k in (1, 2, 3)]
    rings[0].launch()

    for n in range(4):
        own_block(c, y, n)
    came_all(gq.at[0, 0:3], gr.at[2])
    group_c.start()
    other_blocks()
    launch_x(0)
    for copy in keep(c, 1):
        copy.start()
    rest()
    keep_other.wait()
    rings[0].relay()
    for k in (1, 3, 2):
        piece_x(1, k, 0, HALF, 6).wait_recv()
        rings[k].launch()
    relay_x(0)
    rings[0].finish()
    for k in (1, 3, 2):
        rings[k].relay()
    finish_x(0, (0, 1))
    rings[1].finish()
    rings[3].finish()
    finish_x(0, (2, 3))
    rings[2].finish()

    all_sent(11, gq.at[0])
    came_all(params.at[0:7 * HALF, :], kr.at[0])
    all_sent(12, params.at[0:27 * 64, :])
    all_sent(13, params.at[0:7 * HALF, :])
    for copy in keep(c, 1) + keep(1 - c, 6):
        copy.wait()
    for wait in left:
        wait()


def store(*refs):
    copies = [pltpu.make_async_copy(refs[n], refs[5 + n], refs[10].at[n]) for n in range(5)]
    for copy in copies[::-1]:
        copy.start()
    for copy in copies:
        copy.wait()


def shards(activations, out_grad, master, moment_one, moment_two, alive, step_count):
    hbm = pl.BlockSpec(memory_space=pl.ANY)
    dma = pltpu.SemaphoreType.DMA
    vm = pltpu.VMEM
    results = [((SH, KVW), F32)] * 4 + [((DW, KVW), BF16)]
    held = pl.pallas_call(
        kernel,
        out_shape=[vm(*r) for r in results],
        in_specs=[hbm] * 6 + [pl.BlockSpec(memory_space=pltpu.SMEM)],
        out_specs=[hbm] * 5,
        scratch_shapes=[
            vm((SH, KVW), F32), vm((SH, KVW), F32), vm((SH, KVW), F32), vm((SH, KVW), F32),
            vm((SH, KVW), BF16), vm((HALF, 128), BF16),
            vm((TOK, DW), BF16), vm((TOK, KVW), BF16),
            vm((SH, KVW), F32), vm((SH, KVW), F32), vm((SH, KVW), F32), vm((3, HALF, 128), F32),
            vm((8, SH, KVW), F32), vm((8, QR, KVW), I16), vm((8, QR, KVW), I16), vm((8, HALF, KVW), F32),
            vm((8, QR, KVW), I16), vm((8, QR, KVW), I16), vm((24, QR, 128), I16),
            vm((2, QR, KVW), I16), vm((2, 3, QR, 128), I16), vm((2, 3, QR, 128), I16),
            vm((HALF, KVW), F32), vm((2, HALF, 128), F32),
            vm((7, 80, 128), I16), vm((7, 80, 128), I16),
            vm((64, 128), F32), vm((2, 4, 4, 80, 128), I16), vm((4, 80, 128), I16),
            vm((8, 8, 128), F32), vm((16, 8, 128), F32), vm((2, 8, 128), F32),
            pltpu.SMEM((32,), jnp.int32),
            dma((13,)), dma((14,)), dma((8,)), dma((8,)), dma((2,)), dma((1,)), dma((1,)), dma((3,)), dma((4,)),
            dma((21,)), dma((1,)), dma((11,)),
        ],
        compiler_params=pltpu.CompilerParams(
            collective_id=0, has_side_effects=True, vmem_limit_bytes=50 * 2**20),
        name="reduce_update_gather",
    )(activations, out_grad, master, moment_one, moment_two, alive, step_count)
    return tuple(pl.pallas_call(
        store,
        out_shape=[jax.ShapeDtypeStruct(*r) for r in results],
        in_specs=[hbm] * 5,
        out_specs=[hbm] * 5,
        scratch_shapes=[dma((5,))],
        compiler_params=pltpu.CompilerParams(vmem_limit_bytes=2**20),
        name="store_results",
    )(*(pltpu.with_memory_space_constraint(v, vm) for v in held)))


def solution(mesh):
    return jax.shard_map(
        shards,
        mesh=mesh,
        in_specs=(
            P(("replica", "shard"), None),
            P(("replica", "shard"), None),
            P("shard", None),
            P("shard", None),
            P("shard", None),
            P(),
            P(),
        ),
        out_specs=(P("shard", None), P("shard", None), P("shard", None), P("shard", None), P()),
        check_vma=False,
    )
```
